512 devices in a mesh: expert: 32 (over y_lo, z), cuts: 16 (over y_hi, x, core).
Axes of the slice: x: 4, y: 4 (y_hi: 2, y_lo: 2; y = y_hi * 2 + y_lo), z: 16, core: 2. Of those that a mesh axis runs over, the one named last changes fastest.
Arguments:
- tokens: bfloat16 [1024, 4096], P('expert', 'cuts'), may hold values from -6 to 6
- expert_ids: int32 [1024, 2], P('expert'), may hold values from 0 to 15, all different within a row; in each aligned block of 32 rows (0 to 31, 32 to 63, ...) at most 8 rows name the same one
- gate_weights: float32 [1024, 2], P('expert'), may hold values from 0.25 to 1
- old_up: bfloat16 [65536, 4096], P('expert', 'cuts'), may hold values from -0.09375 to 0.09375
- old_down: bfloat16 [65536, 4096], P('expert', 'cuts'), may hold values from -0.09375 to 0.09375
- old_rows: int32 [16], replicated, may hold values from 0 to 15, each once
- new_slots: int32 [16], replicated, may hold values from 0 to 15, each once
- cotangent: bfloat16 [1024, 4096], P('expert', 'cuts'), may hold values from -6 to 6
Outputs:
- mixed: bfloat16 [1024, 4096], P('expert', 'cuts')
- token_grad: bfloat16 [1024, 4096], P('expert', 'cuts')
- up_grad: bfloat16 [65536, 4096], P(('expert', 'cuts'))
- down_grad: bfloat16 [65536, 4096], P(('expert', 'cuts'))
The draws below stay inside these ranges and needn't reach their ends.
Inputs may be any that keep to these rules, and one draw needn't show every extreme that they name: `expert_ids`: each row names two different experts; in each aligned block of 32 rows (the rows of one index of the expert axis) no expert is named more than 8 times, and in some blocks one expert exactly 8 times. `old_rows`: each number once. `new_slots`: each number once.
All inputs are finite; a program needn't handle non-finite values.
Results may differ from the reference program's by a relative error of at most 0.02.
Values may be sent and summed in bfloat16 or wider, within the bound.
No kernel may reach another device: no remote copies, remote signals or barrier semaphores. Data moves between devices by JAX's collectives and lax.ppermute only.
A program may use at most 64 MiB of HBM per device.

```python
import math
import jax
import jax.numpy as jnp
import numpy as np
from jax import lax

D = 4096
FF = 4096
TOK_DEV = 32
EXPERTS = 16
CAP = 8
TOKENS = 1024
N_EXPERT = 32
N_CUTS = 16


def level_of(own_key, extent, cuts, low, top_value):
    gain, own = 1.0, jax.random.fold_in(own_key, 6)
    for position, parts in cuts:
        heights = jnp.exp(jax.random.uniform(jax.random.fold_in(own, position), (parts,), jnp.float32, low / len(cuts), top_value / len(cuts)))
        gain = gain * jnp.repeat(heights, extent[position] // parts).reshape([-1 if axis == position else 1 for axis in range(len(extent))])
    return gain


def assign_block(rng, own, number, rows, number_of, top, reach, slope):
    sequence = jax.random.permutation(rng, number_of)
    heavy_load, ordinary = shares(number_of, rows * top, reach, slope, True), shares(number_of, rows * top, reach, slope, False)
    places = jnp.arange(number_of)

    def named(sizes, turn):
        used = int((sizes > 0).sum())
        fixed = max(1, used // 4)
        passed = fixed + (places - fixed + turn * (used - fixed)) % max(1, number_of - fixed)
        return jnp.zeros((number_of,), jnp.int32).at[sequence[jnp.where(places < fixed, places, passed)]].set(jnp.asarray(sizes, jnp.int32))

    sizes = jnp.where(number % 4 == 0, named(heavy_load, number // 4), named(ordinary, number - number // 4 - 1))
    mixed = jax.random.permutation(jax.random.fold_in(own, 3), number_of)
    giver, sink = mixed[0:number_of // 2 * 2:2], mixed[1:number_of // 2 * 2:2]
    slack = jnp.minimum(sizes[giver] - 1, reach - sizes[sink]) // 2
    slack = jnp.where((giver == sequence[0]) | (sink == sequence[0]) | (sizes[sink] == 0), 0, jnp.maximum(slack, 0))
    passed = jax.random.randint(jax.random.fold_in(own, 4), (number_of // 2,), 0, 1 << 20) % (slack + 1)
    sizes = sizes.at[giver].add(-passed).at[sink].add(passed)
    members = jnp.searchsorted(jnp.cumsum(sizes), jnp.arange(rows * top), side="right").astype(jnp.int32)
    grid = members.reshape(top, rows).T
    grid = grid[jax.random.permutation(jax.random.fold_in(own, 1), rows)]
    turn = jax.random.randint(jax.random.fold_in(own, 2), (rows, 1), 0, top)
    return jnp.take_along_axis(grid, (jnp.arange(top)[None, :] + turn) % top, axis=1)


def shares(amount, total, most, slope, full):
    weights = [(1 << 20) // math.isqrt(rank ** slope) + 1 for rank in range(1, amount + 1)]
    largest = most if full else min(most, max(-(-total // amount), total * weights[0] // sum(weights)))
    least = 1 if total - largest >= amount - 1 else 0
    given, surplus = [largest] + [least] * (amount - 1), total - largest - least * (amount - 1)
    while surplus > 0:
        candidates = [i for i in range(1, amount) if given[i] < largest] or [i for i in range(1, amount) if given[i] < most]
        whole, left = sum([weights[i] for i in candidates]), surplus
        for i in candidates:
            addition = min(most - given[i], max(1, left * weights[i] // whole), surplus)
            given[i] = given[i] + addition
            surplus = surplus - addition
    return np.array(given)


def normal_values(key, dims, deviation, reach, cuts=(), held_as=jnp.bfloat16):
    drawn = jax.random.normal(key, dims, jnp.float32) * deviation
    if len(cuts) > 0:
        drawn = level_of(key, dims, cuts, -0.22, 0.18) * drawn
    return jnp.clip(drawn, min=-reach, max=reach).astype(held_as)


def setup_inputs(seed: int = 0) -> dict:
    key_of = jax.random.split(jax.random.key(seed), 9)
    tokens = normal_values(key_of[0], (TOKENS, D), 1.0, 6.0, ((0, 32), (1, 16)))
    expert_ids_keys = jax.random.split(jax.random.fold_in(key_of[1], 1), TOKENS // TOK_DEV)
    expert_ids_turns = jax.random.permutation(jax.random.fold_in(key_of[1], 3), TOKENS // TOK_DEV)
    expert_ids = jax.vmap(lambda own, number: assign_block(jax.random.fold_in(key_of[1], 2), own, number, TOK_DEV, EXPERTS, 2, CAP, 2))(expert_ids_keys, expert_ids_turns).reshape((TOKENS, 2))
    gate_weights = jnp.clip(0.25 + 0.75 * jax.random.uniform(key_of[2], (TOKENS, 2), jnp.float32) ** level_of(key_of[2], (TOKENS, 2), ((0, 32),), -0.2, 0.2), 0.25, 1.0)
    old_up = normal_values(key_of[3], (EXPERTS * FF, D), D ** -0.5, 0.09375, ((0, 32), (1, 16)))
    old_down = normal_values(key_of[4], (EXPERTS * FF, D), FF ** -0.5, 0.09375, ((0, 32), (1, 16)))
    old_rows = jax.random.permutation(key_of[5], N_CUTS).astype(jnp.int32)
    new_slots = jax.random.permutation(key_of[6], N_CUTS).astype(jnp.int32)
    cotangent = normal_values(key_of[7], (TOKENS, D), 1.0, 6.0, ((0, 32), (1, 16)))
    return {"tokens": tokens, "expert_ids": expert_ids, "gate_weights": gate_weights, "old_up": old_up, "old_down": old_down, "old_rows": old_rows, "new_slots": new_slots, "cotangent": cotangent}


def relabel(stored, old_rows):
    block_width = D // N_CUTS
    pieces = stored.reshape(EXPERTS, FF, N_CUTS, block_width)
    placed = jnp.zeros_like(pieces).at[:, :, old_rows].set(pieces)
    return placed.reshape(EXPERTS, FF, D)


def to_slots(grads, new_slots):
    unit_width = FF // (2 * N_CUTS)
    shaped = grads.reshape(EXPERTS, 2, N_CUTS, unit_width, D)
    return jnp.take(shaped, new_slots, axis=2).reshape(EXPERTS * FF, D)


def block_sums(left, right_mat, slots):
    unit_width = FF // (2 * N_CUTS)
    left_blocks = left.astype(jnp.float32).reshape(slots, 2 * N_CUTS, unit_width)
    right_blocks = right_mat.astype(jnp.float32).reshape(2 * N_CUTS, unit_width, D)
    pieces = jnp.einsum("sju,jud->sjd", left_blocks, right_blocks, precision=lax.Precision.HIGHEST).astype(jnp.bfloat16)
    halves = jnp.sum(pieces.astype(jnp.float32).reshape(slots, 2, N_CUTS, D), axis=2).astype(jnp.bfloat16)
    return halves[:, 0].astype(jnp.float32) + halves[:, 1].astype(jnp.float32)


def reference(tokens, expert_ids, gate_weights, old_up, old_down, old_rows, new_slots, cotangent):
    slots = N_EXPERT * CAP
    up_true = relabel(old_up, old_rows)
    down_true = relabel(old_down, old_rows)
    flat_ids = expert_ids.reshape(-1).astype(jnp.int32)
    flat_gate = gate_weights.reshape(-1).astype(jnp.float32)
    back_all = (gate_weights[:, :, None].astype(jnp.float32) * cotangent[:, None, :].astype(jnp.float32)).astype(jnp.bfloat16).reshape(2 * TOKENS, D)

    def per_expert(carry, inputs):
        mixed_acc, grad_acc = carry
        expert, up_mat, down_mat = inputs
        picked = jnp.argsort((flat_ids != expert).astype(jnp.int32), stable=True)[:slots].astype(jnp.int32)
        is_live = (flat_ids[picked] == expert)
        token_rows = (picked // 2).astype(jnp.int32)
        picked_x = tokens[token_rows] * is_live[:, None].astype(jnp.bfloat16)
        picked_back = back_all[picked] * is_live[:, None].astype(jnp.bfloat16)
        gate_vals = flat_gate[picked] * is_live.astype(jnp.float32)
        pre_act = jnp.dot(picked_x, up_mat.T, preferred_element_type=jnp.float32)
        hidden = jax.nn.silu(pre_act).astype(jnp.bfloat16)
        out_rows = gate_vals[:, None] * block_sums(hidden, down_mat, slots)
        mixed_acc = mixed_acc.at[token_rows].add(out_rows)
        sigmoid_val = jax.nn.sigmoid(pre_act)
        hidden_grad = jnp.dot(picked_back, down_mat.T, preferred_element_type=jnp.float32)
        pre_grad = (hidden_grad * sigmoid_val * (1.0 + pre_act * (1.0 - sigmoid_val))).astype(jnp.bfloat16)
        grad_rows = block_sums(pre_grad, up_mat, slots) * is_live[:, None].astype(jnp.float32)
        grad_acc = grad_acc.at[token_rows].add(grad_rows)
        up_part = jnp.dot(pre_grad.T, picked_x, preferred_element_type=jnp.float32).astype(jnp.bfloat16)
        down_part = jnp.dot(hidden.T, picked_back, preferred_element_type=jnp.float32).astype(jnp.bfloat16)
        return (mixed_acc, grad_acc), (up_part, down_part)

    start = (jnp.zeros((TOKENS, D), jnp.float32), jnp.zeros((TOKENS, D), jnp.float32))
    expert_list = jnp.arange(EXPERTS).astype(jnp.int32)
    (mixed_acc, grad_acc), (up_all, down_all) = lax.scan(per_expert, start, (expert_list, up_true, down_true))
    mixed = mixed_acc.astype(jnp.bfloat16)
    token_grad = grad_acc.astype(jnp.bfloat16)
    return mixed, token_grad, to_slots(up_all, new_slots), to_slots(down_all, new_slots)
```

```python
import jax
import jax.numpy as jnp
from jax import lax
from jax.sharding import PartitionSpec as P

F32, BF16 = jnp.float32, jnp.bfloat16


def exchange(parts, axis):
    return lax.all_to_all(parts, axis, split_axis=0, concat_axis=0, tiled=True)


def everywhere(block, axis):
    return exchange(jnp.broadcast_to(block[None], (lax.axis_size(axis), *block.shape)), axis)


def local(tokens, expert_ids, gate_weights, old_up, old_down, old_rows, new_slots, cotangent):
    cut_count = lax.axis_size("cuts")
    group_count = lax.axis_size("expert")
    expert_count = group_count // 2
    tok_rows, block_width = tokens.shape
    half_units = old_up.shape[0]
    unit_width = half_units // cut_count
    capacity = 8 * tok_rows // group_count
    slot_rows = group_count * capacity
    cut = lax.axis_index("cuts")
    own_block = lax.dynamic_index_in_dim(old_rows, cut, keepdims=False)
    cut_list = jnp.arange(cut_count, dtype=jnp.int32)
    inverse = jnp.sum(
        cut_list[:, None] * (old_rows[:, None] == cut_list[None, :]).astype(jnp.int32), axis=0
    )
    own_source = jnp.sum(cut_list * (old_rows == cut).astype(jnp.int32))

    with jax.named_scope("token_blocks"):
        both = everywhere(jnp.concatenate([tokens, cotangent], axis=1), "cuts")
        both = lax.dynamic_index_in_dim(both, own_block, axis=0, keepdims=False)

    flat_ids = expert_ids.reshape(-1)
    expert_hits = (flat_ids[:, None] == jnp.arange(expert_count, dtype=jnp.int32)[None, :]).astype(
        jnp.int32
    )
    slot_rank = jnp.sum((jnp.cumsum(expert_hits, axis=0) - expert_hits) * expert_hits, axis=1)
    target = (flat_ids * capacity + slot_rank).reshape(tok_rows, 2)
    slots = expert_count * capacity
    slot_list = jnp.arange(slots, dtype=jnp.int32)
    matches = slot_list[:, None, None] == target[None]
    placer = jnp.any(matches, axis=2).astype(BF16)
    slot_gate = jnp.sum(jnp.where(matches, gate_weights[None], 0.0), axis=(1, 2))

    with jax.named_scope("dispatch"):
        placed = jnp.dot(placer, both, preferred_element_type=F32)
        scale = jnp.where(
            jnp.arange(2 * block_width)[None, :] < block_width, 1.0, slot_gate[:, None]
        )
        placed = (placed * scale).astype(BF16).reshape(expert_count, 1, capacity, 2 * block_width)
        placed = jnp.broadcast_to(placed, (expert_count, 2, capacity, 2 * block_width))
        routed = exchange(placed.reshape(group_count, capacity, 2 * block_width), "expert")
        routed = routed.reshape(slot_rows, 2 * block_width)
        routed_x, routed_back = routed[:, :block_width], routed[:, block_width:]

    def summed(weights, rows):
        part = lax.dot_general(
            weights, rows, (((1,), (1,)), ((), ())), preferred_element_type=F32
        ).astype(BF16)
        part = exchange(part.reshape(cut_count, unit_width, slot_rows), "cuts")
        return jnp.sum(part.astype(F32), axis=0)

    with jax.named_scope("pre_act"):
        pre_act = summed(old_up, routed_x)
    with jax.named_scope("hidden_grad"):
        hidden_grad = summed(old_down, routed_back)
    with jax.named_scope("hidden"):
        hidden = jax.nn.silu(pre_act).astype(BF16)
        hidden = everywhere(hidden, "cuts").reshape(half_units, slot_rows)
    with jax.named_scope("pre_grad"):
        sig = jax.nn.sigmoid(pre_act)
        pre_grad = (hidden_grad * sig * (1.0 + pre_act * (1.0 - sig))).astype(BF16)
        pre_grad = everywhere(pre_grad, "cuts").reshape(half_units, slot_rows)

    def rows_of(units, weights):
        return lax.dot_general(
            units, weights, (((0,), (0,)), ((), ())), preferred_element_type=F32
        ).astype(BF16)

    with jax.named_scope("give_back"):
        half_rows = jnp.concatenate(
            [rows_of(hidden, old_down), rows_of(pre_grad, old_up)], axis=1
        ).reshape(group_count, capacity, 2 * block_width)
        half_rows = exchange(half_rows, "expert").reshape(slot_rows, 2 * block_width)
        row_list = jnp.arange(slot_rows, dtype=jnp.int32)
        row_slot = row_list // (2 * capacity) * capacity + row_list % capacity
        picker = (target.reshape(-1)[:, None] == row_slot[None, :]).astype(BF16)
        entries = jnp.dot(picker, half_rows, preferred_element_type=F32)
        entries = entries.reshape(tok_rows, 2, 2 * block_width)
        mixed = jnp.sum(entries[:, :, :block_width] * gate_weights[:, :, None], axis=1)
        token_grad = jnp.sum(entries[:, :, block_width:], axis=1)
        result = jnp.concatenate([mixed, token_grad], axis=1).astype(BF16)
        result = everywhere(result, "cuts")
        result = lax.dynamic_index_in_dim(result, own_source, axis=0, keepdims=False)

    def new_slices(units, rows):
        grad = jnp.dot(units, rows, preferred_element_type=F32).astype(BF16)
        grad = jnp.take(grad.reshape(cut_count, unit_width, block_width), new_slots, axis=0)
        grad = jnp.take(exchange(grad, "cuts"), inverse, axis=0)
        return jnp.transpose(grad, (1, 0, 2)).reshape(unit_width, cut_count * block_width)

    with jax.named_scope("down_grad"):
        down_grad = new_slices(hidden, routed_back)
    with jax.named_scope("up_grad"):
        up_grad = new_slices(pre_grad, routed_x)
    return (result[:, :block_width], result[:, block_width:], up_grad, down_grad)


def solution(mesh):
    placed = (
        P("expert", "cuts"),
        P("expert", None),
        P("expert", None),
        P("expert", "cuts"),
        P("expert", "cuts"),
        P(),
        P(),
        P("expert", "cuts"),
    )
    return jax.shard_map(
        local,
        mesh=mesh,
        in_specs=placed,
        out_specs=(
            P("expert", "cuts"),
            P("expert", "cuts"),
            P(("expert", "cuts"), None),
            P(("expert", "cuts"), None),
        ),
        check_vma=False,
    )
```

```python
import jax
import jax.numpy as jnp
from jax import lax
from jax.sharding import Mesh, PartitionSpec as P

F32, BF16 = jnp.float32, jnp.bfloat16


def exchange(parts, axis):
    return lax.all_to_all(parts, axis, split_axis=0, concat_axis=0, tiled=True)


def everywhere(block, axis):
    return exchange(jnp.broadcast_to(block[None], (lax.axis_size(axis), *block.shape)), axis)


def swap(block):
    return lax.ppermute(block, "core", [(0, 1), (1, 0)])


def pick(blocks, index):
    return lax.dynamic_index_in_dim(blocks, index, axis=0, keepdims=False)


def rows_at(blocks, places):
    return jnp.take(blocks, places, axis=0, mode="clip")


def local(tokens, expert_ids, gate_weights, old_up, old_down, old_rows, new_slots, cotangent):
    chips = lax.axis_size("chip")
    cut_count = 2 * chips
    group_count = lax.axis_size("expert")
    expert_count = group_count // 2
    tok_rows, width = tokens.shape
    half_units = old_up.shape[0]
    unit_width = half_units // cut_count
    core_units = half_units // 2
    capacity = 8 * tok_rows // group_count
    slot_rows = group_count * capacity
    chip, core = lax.axis_index("chip"), lax.axis_index("core")
    cut = 2 * chip + core
    cut_list = jnp.arange(cut_count, dtype=jnp.int32)
    inverse = jnp.sum(
        cut_list[:, None] * (old_rows[:, None] == cut_list[None, :]).astype(jnp.int32), axis=0
    )
    own_block, other_block = pick(old_rows, cut), pick(old_rows, 2 * chip + 1 - core)
    own_source = pick(inverse, cut)
    other_source = pick(inverse, 2 * chip + 1 - core)

    def across(blocks, own, other):
        theirs = swap(pick(blocks, other // 2))
        return jnp.where(own % 2 == core, pick(blocks, own // 2), theirs)

    slot_pairs = new_slots.reshape(chips, 2)
    kept, given = slot_pairs[:, core], slot_pairs[:, 1 - core]

    def both_blocks(weights):
        blocks = weights.reshape(cut_count, unit_width, width)
        mine, theirs = rows_at(blocks, kept), swap(rows_at(blocks, given))
        return jnp.concatenate([mine, theirs], axis=2).reshape(core_units, 2 * width)

    with jax.named_scope("weights"):
        up, down = both_blocks(old_up), both_blocks(old_down)

    with jax.named_scope("token_blocks"):
        both = everywhere(jnp.concatenate([tokens, cotangent], axis=1), "chip")
        both = across(both, own_block, other_block)

    flat_ids = expert_ids.reshape(-1)
    expert_hits = (flat_ids[:, None] == jnp.arange(expert_count, dtype=jnp.int32)[None, :]).astype(
        jnp.int32
    )
    slot_rank = jnp.sum((jnp.cumsum(expert_hits, axis=0) - expert_hits) * expert_hits, axis=1)
    target = (flat_ids * capacity + slot_rank).reshape(tok_rows, 2)
    slots = expert_count * capacity
    slot_list = jnp.arange(slots, dtype=jnp.int32)
    matches = slot_list[:, None, None] == target[None]
    placer = jnp.any(matches, axis=2).astype(BF16)
    slot_gate = jnp.sum(jnp.where(matches, gate_weights[None], 0.0), axis=(1, 2))

    with jax.named_scope("dispatch"):
        placed = jnp.dot(placer, both, preferred_element_type=F32)
        scale = jnp.where(jnp.arange(2 * width)[None, :] < width, 1.0, slot_gate[:, None])
        placed = (placed * scale).astype(BF16).reshape(expert_count, 1, capacity, 2 * width)
        placed = jnp.broadcast_to(placed, (expert_count, 2, capacity, 2 * width))
        routed = exchange(placed.reshape(group_count, capacity, 2 * width), "expert")
        routed = routed.reshape(slot_rows, 2 * width)
        other = swap(routed)
        routed_x = jnp.concatenate([routed[:, :width], other[:, :width]], axis=1)
        routed_back = jnp.concatenate([routed[:, width:], other[:, width:]], axis=1)

    def partial(weights, rows):
        part = lax.dot_general(
            weights, rows, (((1,), (1,)), ((), ())), preferred_element_type=F32
        ).astype(BF16)
        return part.reshape(chips, unit_width, slot_rows)

    with jax.named_scope("hidden"):
        parts = jnp.concatenate([partial(up, routed_x), partial(down, routed_back)], axis=1)
        sums = jnp.sum(exchange(parts, "chip").astype(F32), axis=0)
        pre_act, hidden_grad = sums[:unit_width], sums[unit_width:]
        sig = jax.nn.sigmoid(pre_act)
        hidden = jax.nn.silu(pre_act).astype(BF16)
        pre_grad = (hidden_grad * sig * (1.0 + pre_act * (1.0 - sig))).astype(BF16)
        units = everywhere(jnp.concatenate([hidden, pre_grad], axis=0), "chip")
        hidden = units[:, :unit_width].reshape(core_units, slot_rows)
        pre_grad = units[:, unit_width:].reshape(core_units, slot_rows)

    def rows_of(units, weights):
        return lax.dot_general(
            units, weights, (((0,), (0,)), ((), ())), preferred_element_type=F32
        )

    with jax.named_scope("give_back"):
        out_part, in_part = rows_of(hidden, down), rows_of(pre_grad, up)
        theirs = swap(jnp.concatenate([out_part[:, width:], in_part[:, width:]], axis=1).astype(BF16))
        own = jnp.concatenate([out_part[:, :width], in_part[:, :width]], axis=1)
        half_rows = (own + theirs.astype(F32)).astype(BF16)
        half_rows = exchange(half_rows.reshape(group_count, capacity, 2 * width), "expert")
        row_list = jnp.arange(slot_rows, dtype=jnp.int32)
        row_slot = row_list // (2 * capacity) * capacity + row_list % capacity
        picker = (target.reshape(-1)[:, None] == row_slot[None, :]).astype(BF16)
        entries = jnp.dot(picker, half_rows.reshape(slot_rows, 2 * width), preferred_element_type=F32)
        entries = entries.reshape(tok_rows, 2, 2 * width)
        mixed = jnp.sum(entries[:, :, :width] * gate_weights[:, :, None], axis=1)
        token_grad = jnp.sum(entries[:, :, width:], axis=1)
        result = jnp.concatenate([mixed, token_grad], axis=1).astype(BF16)

    def outer(units, rows):
        grad = jnp.dot(units, rows, preferred_element_type=F32).astype(BF16)
        return grad.reshape(chips, unit_width, 2 * width)

    with jax.named_scope("new_slices"):
        result = jnp.broadcast_to(result[None], (chips, tok_rows, 2 * width))
        sent = jnp.concatenate([outer(pre_grad, routed_x), outer(hidden, routed_back), result], axis=1)
        got = exchange(sent, "chip")
        result = across(got[:, 2 * unit_width :], own_source, other_source)

        def place(grad):
            grad = grad.reshape(chips, unit_width, 2, width).transpose(0, 2, 1, 3)
            grad = grad.reshape(cut_count, unit_width, width)
            source = inverse // 2 * 2 + (inverse % 2 != core).astype(jnp.int32)
            grad = rows_at(grad, source)
            return jnp.transpose(grad, (1, 0, 2)).reshape(unit_width, cut_count * width)

        up_grad, down_grad = place(got[:, :unit_width]), place(got[:, unit_width : 2 * unit_width])
    return (result[:, :width], result[:, width:], up_grad, down_grad)


def solution(mesh):
    experts, cuts = mesh.devices.shape
    split = Mesh(mesh.devices.reshape(experts, cuts // 2, 2), ("expert", "chip", "core"))
    spread = P("expert", ("chip", "core"))
    return jax.shard_map(
        local,
        mesh=split,
        in_specs=(spread, P("expert", None), P("expert", None), spread, spread, P(), P(), spread),
        out_specs=(
            spread,
            spread,
            P(("expert", "chip", "core"), None),
            P(("expert", "chip", "core"), None),
        ),
        check_vma=False,
    )
```

```python
import jax
import jax.numpy as jnp
from jax import lax
from jax.experimental import pallas as pl
from jax.experimental.pallas import tpu as pltpu
from jax.sharding import Mesh, PartitionSpec as P

F32, BF16 = jnp.float32, jnp.bfloat16
CHIP = ("y", "x")
CUTS = ("y", "x", "core")
VMEM = pl.BlockSpec(memory_space=pltpu.VMEM)


def exchange(parts, axis):
    return lax.all_to_all(parts, axis, split_axis=0, concat_axis=0, tiled=True)


def everywhere(block, axis):
    count = lax.axis_size(axis)
    return exchange(jnp.broadcast_to(block[None], (count, *block.shape)), axis)


def swap(block):
    return lax.ppermute(block, "core", [(0, 1), (1, 0)])


def pick(blocks, index):
    return lax.dynamic_index_in_dim(blocks, index, axis=0, keepdims=False)


def rows_at(blocks, places):
    return jnp.take(blocks, places, axis=0, mode="clip")


def transposed_dot(left, right):
    return lax.dot_general(left, right, (((0,), (0,)), ((), ())), preferred_element_type=F32)


def place_kernel(capacity, ids_ref, gate_ref, token_ref, cotangent_ref, rows_ref, picker_ref):
    tok_rows, width = token_ref.shape
    slot_rows = rows_ref.shape[0]
    ids, gates = ids_ref[...], gate_ref[...]
    lane = lax.broadcasted_iota(jnp.int32, (tok_rows, 128), 1)
    hits = [(ids[:, k : k + 1] == lane).astype(F32) for k in range(2)]
    earlier = lax.broadcasted_iota(jnp.int32, (tok_rows, tok_rows), 0) > (
        lax.broadcasted_iota(jnp.int32, (tok_rows, tok_rows), 1)
    )
    before = jnp.dot(
        earlier.astype(BF16), (hits[0] + hits[1]).astype(BF16), preferred_element_type=F32
    )
    row = lax.broadcasted_iota(jnp.int32, (tok_rows, slot_rows), 1)
    within = row & (capacity - 1)
    row_slot = ((row & -(2 * capacity)) >> 1) + within
    pickers = []
    for k in range(2):
        rank = jnp.sum(before * hits[k], axis=1, keepdims=True).astype(jnp.int32)
        target = ids[:, k : k + 1] * capacity + rank
        pickers.append((target == row_slot).astype(BF16))
        picker_ref[k] = pickers[k]
    rows_ref[:, :width] = transposed_dot(pickers[0] + pickers[1], token_ref[...]).astype(BF16)
    back = jnp.zeros((slot_rows, width), F32)
    for k in range(2):
        scaled = gates[:, k : k + 1] * cotangent_ref[...].astype(F32)
        back = back + transposed_dot(pickers[k], scaled.astype(BF16))
    rows_ref[:, width:] = back.astype(BF16)


def combine_kernel(rows_ref, picker_ref, gate_ref, result_ref):
    width = rows_ref.shape[1] // 2
    gates = gate_ref[...]
    rows = rows_ref[...]
    entries = [jnp.dot(picker_ref[k], rows, preferred_element_type=F32) for k in range(2)]
    mixed = gates[:, 0:1] * entries[0][:, :width] + gates[:, 1:2] * entries[1][:, :width]
    token_grad = entries[0][:, width:] + entries[1][:, width:]
    for copy in range(result_ref.shape[0]):
        result_ref[copy, :, :width] = mixed.astype(BF16)
        result_ref[copy, :, width:] = token_grad.astype(BF16)


def local(tokens, expert_ids, gate_weights, old_up, old_down, old_rows, new_slots, cotangent):
    chips = lax.axis_size(CHIP)
    cut_count = 2 * chips
    group_count = lax.axis_size("expert")
    tok_rows, width = tokens.shape
    half_units = old_up.shape[0]
    unit_width = half_units // cut_count
    core_units = half_units // 2
    capacity = 8 * tok_rows // group_count
    slot_rows = group_count * capacity
    chip, core = lax.axis_index(CHIP), lax.axis_index("core")
    cut = 2 * chip + core
    own_source = jnp.sum(
        jnp.arange(cut_count, dtype=jnp.int32) * (old_rows == cut).astype(jnp.int32)
    )

    with jax.named_scope("dispatch"):
        rows, pickers = pl.pallas_call(
            lambda *refs: place_kernel(capacity, *refs),
            out_shape=(
                jax.ShapeDtypeStruct((slot_rows, 2 * width), BF16),
                jax.ShapeDtypeStruct((2, tok_rows, slot_rows), BF16),
            ),
            in_specs=[VMEM] * 4,
            out_specs=(VMEM, VMEM),
        )(expert_ids, gate_weights, tokens, cotangent)
        rows = exchange(rows.reshape(group_count, capacity, 2 * width), "expert")
        rows = rows.reshape(slot_rows, 2 * width)

    slot_pairs = new_slots.reshape(chips, 2)
    kept, given = slot_pairs[:, core], slot_pairs[:, 1 - core]

    def both_blocks(weights):
        blocks = weights.reshape(cut_count, unit_width, width)
        mine, theirs = rows_at(blocks, kept), swap(rows_at(blocks, given))
        return jnp.concatenate([mine, theirs], axis=2).reshape(core_units, 2 * width)

    with jax.named_scope("weights"):
        up, down = both_blocks(old_up), both_blocks(old_down)

    with jax.named_scope("all_rows"):
        all_rows = everywhere(rows, CHIP)
        needed = [pick(old_rows, cut), pick(old_rows, 2 * chip + 1 - core)]
        mine = [pick(all_rows, block // 2) for block in needed]
        theirs = swap(jnp.concatenate([mine[1], mine[0]], axis=1))
        chosen = [
            jnp.where(block % 2 == core, mine[j], theirs[:, 2 * width * j : 2 * width * (j + 1)])
            for j, block in enumerate(needed)
        ]
        routed_x = jnp.concatenate([rows[:, :width] for rows in chosen], axis=1)
        routed_back = jnp.concatenate([rows[:, width:] for rows in chosen], axis=1)

    def partial(weights, rows):
        part = lax.dot_general(
            weights, rows, (((1,), (1,)), ((), ())), preferred_element_type=F32
        ).astype(BF16)
        return part.reshape(chips, unit_width, slot_rows)

    with jax.named_scope("hidden"):
        parts = jnp.concatenate([partial(up, routed_x), partial(down, routed_back)], axis=1)
        sums = jnp.sum(exchange(parts, CHIP).astype(F32), axis=0)
        pre_act, hidden_grad = sums[:unit_width], sums[unit_width:]
        sig = jax.nn.sigmoid(pre_act)
        hidden = jax.nn.silu(pre_act).astype(BF16)
        pre_grad = (hidden_grad * sig * (1.0 + pre_act * (1.0 - sig))).astype(BF16)
        own_units = jnp.concatenate([hidden, pre_grad], axis=0)
        other_units = swap(own_units)
        units = everywhere(own_units, CHIP)
        hidden = units[:, :unit_width].reshape(core_units, slot_rows)
        pre_grad = units[:, unit_width:].reshape(core_units, slot_rows)

    with jax.named_scope("give_back"):
        out_part, in_part = transposed_dot(hidden, down), transposed_dot(pre_grad, up)
        theirs = swap(jnp.concatenate([out_part[:, width:], in_part[:, width:]], axis=1).astype(BF16))
        own = jnp.concatenate([out_part[:, :width], in_part[:, :width]], axis=1)
        half_rows = (own + theirs.astype(F32)).astype(BF16)
        half_rows = exchange(half_rows.reshape(group_count, capacity, 2 * width), "expert")
        result = pl.pallas_call(
            combine_kernel,
            out_shape=jax.ShapeDtypeStruct((cut_count, tok_rows, 2 * width), BF16),
            in_specs=[VMEM] * 3,
            out_specs=VMEM,
        )(half_rows.reshape(slot_rows, 2 * width), pickers, gate_weights)

    with jax.named_scope("result"):
        result = pick(exchange(result, CUTS), own_source)

    with jax.named_scope("new_slices"):

        def outer(own, other, rows):
            units = jnp.concatenate([own, other], axis=0)
            return jnp.einsum("ur,brd->bud", units, rows, preferred_element_type=F32).astype(BF16)

        up_part = outer(own_units[unit_width:], other_units[unit_width:], all_rows[:, :, :width])
        down_part = outer(own_units[:unit_width], other_units[:unit_width], all_rows[:, :, width:])
        theirs = swap(jnp.concatenate([up_part[:, unit_width:], down_part[:, unit_width:]], axis=1))

        def place(own, other):
            pair = jnp.where(
                core == 0,
                jnp.concatenate([own, other], axis=2),
                jnp.concatenate([other, own], axis=2),
            )
            return jnp.transpose(pair, (1, 0, 2)).reshape(unit_width, cut_count * width)

        up_grad = place(up_part[:, :unit_width], theirs[:, :unit_width])
        down_grad = place(down_part[:, :unit_width], theirs[:, unit_width:])
    return (result[:, :width], result[:, width:], up_grad, down_grad)


def solution(mesh):
    experts, cuts = mesh.devices.shape
    split = Mesh(mesh.devices.reshape(experts, 2, cuts // 4, 2), ("expert", "y", "x", "core"))
    spread = P("expert", CUTS)
    return jax.shard_map(
        local,
        mesh=split,
        in_specs=(spread, P("expert", None), P("expert", None), spread, spread, P(), P(), spread),
        out_specs=(
            spread,
            spread,
            P(("expert", *CUTS), None),
            P(("expert", *CUTS), None),
        ),
        check_vma=False,
    )
```

```python
import jax
import jax.numpy as jnp
from jax import lax
from jax.experimental import pallas as pl
from jax.experimental.pallas import tpu as pltpu
from jax.sharding import Mesh, PartitionSpec as P

F32, BF16 = jnp.float32, jnp.bfloat16
CHIP = ("y", "x")
CUTS = ("y", "x", "core")
VMEM = pl.BlockSpec(memory_space=pltpu.VMEM)


def exchange(parts, axis):
    return lax.all_to_all(parts, axis, split_axis=0, concat_axis=0, tiled=True)


def swap(block):
    return lax.ppermute(block, "core", [(0, 1), (1, 0)])


def pick(blocks, index):
    return lax.dynamic_index_in_dim(blocks, index, axis=0, keepdims=False)


def rows_at(blocks, places):
    return jnp.take(blocks, places, axis=0, mode="clip")


def transposed_dot(left, right):
    return lax.dot_general(left, right, (((0,), (0,)), ((), ())), preferred_element_type=F32)


def copies_kernel(token_ref, cotangent_ref, copies_ref):
    width = token_ref.shape[1]
    for copy in range(copies_ref.shape[0]):
        copies_ref[copy, :, :width] = token_ref[...]
        copies_ref[copy, :, width:] = cotangent_ref[...]


def place_kernel(capacity, block_ref, ids_ref, gate_ref, blocks_ref, rows_ref, picker_ref):
    tok_rows, width = blocks_ref.shape[1], blocks_ref.shape[2] // 2
    slot_rows = rows_ref.shape[0]
    block = blocks_ref[block_ref[0]]
    ids, gates = ids_ref[...], gate_ref[...]
    lane = lax.broadcasted_iota(jnp.int32, (tok_rows, 128), 1)
    hits = [(ids[:, k : k + 1] == lane).astype(F32) for k in range(2)]
    earlier = lax.broadcasted_iota(jnp.int32, (tok_rows, tok_rows), 0) > (
        lax.broadcasted_iota(jnp.int32, (tok_rows, tok_rows), 1)
    )
    before = jnp.dot(
        earlier.astype(BF16), (hits[0] + hits[1]).astype(BF16), preferred_element_type=F32
    )
    row = lax.broadcasted_iota(jnp.int32, (tok_rows, slot_rows), 1)
    within = row & (capacity - 1)
    row_slot = ((row & -(2 * capacity)) >> 1) + within
    pickers = []
    for k in range(2):
        rank = jnp.sum(before * hits[k], axis=1, keepdims=True).astype(jnp.int32)
        target = ids[:, k : k + 1] * capacity + rank
        pickers.append((target == row_slot).astype(BF16))
        picker_ref[k] = pickers[k]
    rows_ref[:, :width] = transposed_dot(pickers[0] + pickers[1], block[:, :width]).astype(BF16)
    back = jnp.zeros((slot_rows, width), F32)
    for k in range(2):
        scaled = gates[:, k : k + 1] * block[:, width:].astype(F32)
        back = back + transposed_dot(pickers[k], scaled.astype(BF16))
    rows_ref[:, width:] = back.astype(BF16)


def units_kernel(parts_ref, units_ref, copies_ref):
    width = parts_ref.shape[1] // 2
    sums = jnp.sum(parts_ref[...].astype(F32), axis=0)
    pre_act, hidden_grad = sums[:width], sums[width:]
    sig = jax.nn.sigmoid(pre_act)
    hidden = (pre_act * sig).astype(BF16)
    pre_grad = (hidden_grad * sig * (1.0 + pre_act * (1.0 - sig))).astype(BF16)
    units_ref[:width] = hidden
    units_ref[width:] = pre_grad
    for copy in range(copies_ref.shape[0]):
        copies_ref[copy, :width] = hidden
        copies_ref[copy, width:] = pre_grad


def combine_kernel(rows_ref, picker_ref, gate_ref, result_ref):
    width = rows_ref.shape[1] // 2
    gates = gate_ref[...]
    rows = rows_ref[...]
    entries = [jnp.dot(picker_ref[k], rows, preferred_element_type=F32) for k in range(2)]
    mixed = gates[:, 0:1] * entries[0][:, :width] + gates[:, 1:2] * entries[1][:, :width]
    token_grad = entries[0][:, width:] + entries[1][:, width:]
    for copy in range(result_ref.shape[0]):
        result_ref[copy, :, :width] = mixed.astype(BF16)
        result_ref[copy, :, width:] = token_grad.astype(BF16)


def local(tokens, expert_ids, gate_weights, old_up, old_down, old_rows, new_slots, cotangent):
    chips = lax.axis_size(CHIP)
    cut_count = 2 * chips
    group_count = lax.axis_size("expert")
    tok_rows, width = tokens.shape
    half_units = old_up.shape[0]
    unit_width = half_units // cut_count
    core_units = half_units // 2
    capacity = 8 * tok_rows // group_count
    slot_rows = group_count * capacity
    chip, core = lax.axis_index(CHIP), lax.axis_index("core")
    cut = 2 * chip + core
    cut_list = jnp.arange(cut_count, dtype=jnp.int32)
    inverse = jnp.sum(
        cut_list[:, None] * (old_rows[:, None] == cut_list[None, :]).astype(jnp.int32), axis=0
    )

    with jax.named_scope("token_blocks"):
        blocks = pl.pallas_call(
            copies_kernel,
            out_shape=jax.ShapeDtypeStruct((cut_count, tok_rows, 2 * width), BF16),
            in_specs=[VMEM] * 2,
            out_specs=VMEM,
        )(tokens, cotangent)
        blocks = exchange(blocks, CUTS)

    with jax.named_scope("dispatch"):
        rows, pickers = pl.pallas_call(
            lambda *refs: place_kernel(capacity, *refs),
            out_shape=(
                jax.ShapeDtypeStruct((slot_rows, 2 * width), BF16),
                jax.ShapeDtypeStruct((2, tok_rows, slot_rows), BF16),
            ),
            in_specs=[pl.BlockSpec(memory_space=pltpu.SMEM)] + [VMEM] * 3,
            out_specs=(VMEM, VMEM),
        )(pick(old_rows, cut).reshape(1), expert_ids, gate_weights, blocks)
        rows = exchange(rows.reshape(group_count, capacity, 2 * width), "expert")
        rows = rows.reshape(slot_rows, 2 * width)
        other = swap(rows)
        routed_x = jnp.concatenate([rows[:, :width], other[:, :width]], axis=1)
        routed_back = jnp.concatenate([rows[:, width:], other[:, width:]], axis=1)

    with jax.named_scope("all_rows"):
        all_rows = lax.all_gather(rows, CHIP)

    slot_pairs = new_slots.reshape(chips, 2)
    kept, given = slot_pairs[:, core], slot_pairs[:, 1 - core]

    def both_blocks(weights):
        blocks = weights.reshape(cut_count, unit_width, width)
        mine, theirs = rows_at(blocks, kept), swap(rows_at(blocks, given))
        return jnp.concatenate([mine, theirs], axis=2).reshape(core_units, 2 * width)

    with jax.named_scope("weights"):
        up, down = both_blocks(old_up), both_blocks(old_down)

    def partial(weights, rows):
        part = lax.dot_general(
            weights, rows, (((1,), (1,)), ((), ())), preferred_element_type=F32
        ).astype(BF16)
        return part.reshape(chips, unit_width, slot_rows)

    with jax.named_scope("hidden"):
        parts = jnp.concatenate([partial(up, routed_x), partial(down, routed_back)], axis=1)
        own_units, copies = pl.pallas_call(
            units_kernel,
            out_shape=(
                jax.ShapeDtypeStruct((2 * unit_width, slot_rows), BF16),
                jax.ShapeDtypeStruct((chips, 2 * unit_width, slot_rows), BF16),
            ),
            in_specs=[VMEM],
            out_specs=(VMEM, VMEM),
        )(exchange(parts, CHIP))
        other_units = swap(own_units)
        units = exchange(copies, CHIP)
        hidden = units[:, :unit_width].reshape(core_units, slot_rows)
        pre_grad = units[:, unit_width:].reshape(core_units, slot_rows)

    with jax.named_scope("give_back"):
        theirs = [transposed_dot(hidden, down[:, width:]), transposed_dot(pre_grad, up[:, width:])]
        theirs = swap(jnp.concatenate([part.astype(BF16) for part in theirs], axis=1))
        own = [transposed_dot(hidden, down[:, :width]), transposed_dot(pre_grad, up[:, :width])]
        half_rows = (jnp.concatenate(own, axis=1) + theirs.astype(F32)).astype(BF16)
        half_rows = exchange(half_rows.reshape(group_count, capacity, 2 * width), "expert")
        result = pl.pallas_call(
            combine_kernel,
            out_shape=jax.ShapeDtypeStruct((cut_count, tok_rows, 2 * width), BF16),
            in_specs=[VMEM] * 3,
            out_specs=VMEM,
        )(half_rows.reshape(slot_rows, 2 * width), pickers, gate_weights)

    with jax.named_scope("result"):
        result = pick(exchange(result, CUTS), pick(inverse, cut))

    with jax.named_scope("new_slices"):

        def outer(own, other, rows):
            units = jnp.concatenate([own, other], axis=0)
            return jnp.einsum("ur,brd->bud", units, rows, preferred_element_type=F32).astype(BF16)

        up_part = outer(own_units[unit_width:], other_units[unit_width:], all_rows[:, :, :width])
        down_part = outer(own_units[:unit_width], other_units[:unit_width], all_rows[:, :, width:])
        theirs = swap(jnp.concatenate([up_part[:, unit_width:], down_part[:, unit_width:]], axis=1))

        source = inverse // 2 + jnp.where(inverse % 2 == core, 0, chips)

        def place(own, other):
            grad = rows_at(jnp.concatenate([own, other], axis=0), source)
            return jnp.transpose(grad, (1, 0, 2)).reshape(unit_width, cut_count * width)

        up_grad = place(up_part[:, :unit_width], theirs[:, :unit_width])
        down_grad = place(down_part[:, :unit_width], theirs[:, unit_width:])
    return (result[:, :width], result[:, width:], up_grad, down_grad)


def solution(mesh):
    experts, cuts = mesh.devices.shape
    split = Mesh(mesh.devices.reshape(experts, 2, cuts // 4, 2), ("expert", "y", "x", "core"))
    spread = P("expert", CUTS)
    return jax.shard_map(
        local,
        mesh=split,
        in_specs=(spread, P("expert", None), P("expert", None), spread, spread, P(), P(), spread),
        out_specs=(
            spread,
            spread,
            P(("expert", *CUTS), None),
            P(("expert", *CUTS), None),
        ),
        check_vma=False,
    )
```

```python
import jax
import jax.numpy as jnp
from jax import lax
from jax.experimental import pallas as pl
from jax.experimental.pallas import tpu as pltpu
from jax.sharding import Mesh, PartitionSpec as P

F32, BF16 = jnp.float32, jnp.bfloat16
CHIP = ("y", "x")
CUTS = ("y", "x", "core")
VMEM = pl.BlockSpec(memory_space=pltpu.VMEM)
ANY = pl.BlockSpec(memory_space=pl.ANY)
LARGE = pltpu.CompilerParams(vmem_limit_bytes=24 * 2**20)


def exchange(parts, axis):
    return lax.all_to_all(parts, axis, split_axis=0, concat_axis=0, tiled=True)


def everywhere(block, axis):
    return exchange(jnp.broadcast_to(block[None], (lax.axis_size(axis), *block.shape)), axis)


def swap(block):
    return lax.ppermute(block, "core", [(0, 1), (1, 0)])


def pick(blocks, index):
    return lax.dynamic_index_in_dim(blocks, index, axis=0, keepdims=False)


def rows_at(blocks, places):
    return jnp.take(blocks, places, axis=0, mode="clip")


def pair_kernel(own_ref, other_ref, after_ref, pair_ref):
    pair_ref[0] = own_ref[...]
    pair_ref[1] = other_ref[...]


def gradient_kernel(*refs):
    own_units, other_units, *rows = refs[:6]
    up_ref, down_ref, their_up, their_down = refs[7:]
    unit_width, width = up_ref.shape[1:]
    units = [
        jnp.concatenate([own_units[part], other_units[part]], axis=0)
        for part in (pl.ds(0, unit_width), pl.ds(unit_width, unit_width))
    ]
    for s, pair in enumerate(rows):
        for t in range(2):
            down = jnp.dot(units[0], pair[t, :, width:], preferred_element_type=F32).astype(BF16)
            up = jnp.dot(units[1], pair[t, :, :width], preferred_element_type=F32).astype(BF16)
            up_ref[2 * s + t] = up[:unit_width]
            down_ref[2 * s + t] = down[:unit_width]
            their_up[2 * s + t] = up[unit_width:]
            their_down[2 * s + t] = down[unit_width:]


def layout_kernel(source_ref, own_up, own_down, their_up, their_down, up_ref, down_ref):
    blocks, unit_width, width = own_up.shape
    for p in range(2 * blocks):
        columns = pl.ds(p * width, width)
        source = source_ref[p]

        @pl.when(source < blocks)
        def _():
            up_ref[:, columns] = own_up[source]
            down_ref[:, columns] = own_down[source]

        @pl.when(source >= blocks)
        def _():
            up_ref[:, columns] = their_up[source - blocks]
            down_ref[:, columns] = their_down[source - blocks]


def local(tokens, expert_ids, gate_weights, old_up, old_down, old_rows, new_slots, cotangent):
    chips = lax.axis_size(CHIP)
    cut_count = 2 * chips
    group_count = lax.axis_size("expert")
    expert_count = group_count // 2
    tok_rows, width = tokens.shape
    half_units = old_up.shape[0]
    unit_width = half_units // cut_count
    core_units = half_units // 2
    capacity = 8 * tok_rows // group_count
    slot_rows = group_count * capacity
    chip, core = lax.axis_index(CHIP), lax.axis_index("core")
    cut = 2 * chip + core
    cut_list = jnp.arange(cut_count, dtype=jnp.int32)
    inverse = jnp.sum(
        cut_list[:, None] * (old_rows[:, None] == cut_list[None, :]).astype(jnp.int32), axis=0
    )
    slot_pairs = new_slots.reshape(chips, 2)
    kept, given = slot_pairs[:, core], slot_pairs[:, 1 - core]

    def both_blocks(weights):
        blocks = weights.reshape(cut_count, unit_width, width)
        mine, theirs = rows_at(blocks, kept), swap(rows_at(blocks, given))
        return jnp.concatenate([mine, theirs], axis=2).reshape(core_units, 2 * width)

    with jax.named_scope("weights"):
        up, down = both_blocks(old_up), both_blocks(old_down)

    with jax.named_scope("token_blocks"):
        both = everywhere(jnp.concatenate([tokens, cotangent], axis=1), CUTS)
        both = pick(both, pick(old_rows, cut))

    flat_ids = expert_ids.reshape(-1)
    expert_hits = (flat_ids[:, None] == jnp.arange(expert_count, dtype=jnp.int32)[None, :]).astype(
        jnp.int32
    )
    slot_rank = jnp.sum((jnp.cumsum(expert_hits, axis=0) - expert_hits) * expert_hits, axis=1)
    target = (flat_ids * capacity + slot_rank).reshape(tok_rows, 2)
    slots = expert_count * capacity
    slot_list = jnp.arange(slots, dtype=jnp.int32)
    matches = slot_list[:, None, None] == target[None]
    placer = jnp.any(matches, axis=2).astype(BF16)
    slot_gate = jnp.sum(jnp.where(matches, gate_weights[None], 0.0), axis=(1, 2))

    with jax.named_scope("dispatch"):
        placed = jnp.dot(placer, both, preferred_element_type=F32)
        scale = jnp.where(jnp.arange(2 * width)[None, :] < width, 1.0, slot_gate[:, None])
        placed = (placed * scale).astype(BF16).reshape(expert_count, 1, capacity, 2 * width)
        placed = jnp.broadcast_to(placed, (expert_count, 2, capacity, 2 * width))
        routed = exchange(placed.reshape(group_count, capacity, 2 * width), "expert")
        routed = routed.reshape(slot_rows, 2 * width)
        other = swap(routed)
        routed_x = jnp.concatenate([routed[:, :width], other[:, :width]], axis=1)
        routed_back = jnp.concatenate([routed[:, width:], other[:, width:]], axis=1)

    def partial(weights, rows):
        part = lax.dot_general(
            weights, rows, (((1,), (1,)), ((), ())), preferred_element_type=F32
        ).astype(BF16)
        return part.reshape(chips, unit_width, slot_rows)

    with jax.named_scope("hidden"):
        parts = jnp.concatenate([partial(up, routed_x), partial(down, routed_back)], axis=1)
        sums = jnp.sum(exchange(parts, CHIP).astype(F32), axis=0)
        pre_act, hidden_grad = sums[:unit_width], sums[unit_width:]
        sig = jax.nn.sigmoid(pre_act)
        hidden = jax.nn.silu(pre_act).astype(BF16)
        pre_grad = (hidden_grad * sig * (1.0 + pre_act * (1.0 - sig))).astype(BF16)
        own_units = jnp.concatenate([hidden, pre_grad], axis=0)
        other_units = swap(own_units)
        early_rows, own_units = lax.optimization_barrier((routed, own_units))
        rows_y = lax.ppermute(early_rows, "y", [(0, 1), (1, 0)])
        units = everywhere(own_units, CHIP)
        units, rows_y, other_units = lax.optimization_barrier((units, rows_y, other_units))
        hidden = units[:, :unit_width].reshape(core_units, slot_rows)
        pre_grad = units[:, unit_width:].reshape(core_units, slot_rows)

    def rows_of(units, weights):
        return lax.dot_general(
            units, weights, (((0,), (0,)), ((), ())), preferred_element_type=F32
        )

    with jax.named_scope("give_back"):
        theirs = [rows_of(hidden, down[:, width:]), rows_of(pre_grad, up[:, width:])]
        theirs = swap(jnp.concatenate([part.astype(BF16) for part in theirs], axis=1))
        own = [rows_of(hidden, down[:, :width]), rows_of(pre_grad, up[:, :width])]
        half_rows = (jnp.concatenate(own, axis=1) + theirs.astype(F32)).astype(BF16)
        sent_rows = half_rows.reshape(group_count, capacity, 2 * width)
        half_rows = exchange(sent_rows, "expert")
        row_list = jnp.arange(slot_rows, dtype=jnp.int32)
        row_slot = row_list // (2 * capacity) * capacity + row_list % capacity
        picker = (target.reshape(-1)[:, None] == row_slot[None, :]).astype(BF16)
        entries = jnp.dot(picker, half_rows.reshape(slot_rows, 2 * width), preferred_element_type=F32)
        entries = entries.reshape(tok_rows, 2, 2 * width)
        mixed = jnp.sum(entries[:, :, :width] * gate_weights[:, :, None], axis=1)
        token_grad = jnp.sum(entries[:, :, width:], axis=1)
        result = jnp.concatenate([mixed, token_grad], axis=1).astype(BF16)

    with jax.named_scope("result"):
        own_result = result
        result = pick(everywhere(own_result, CUTS), pick(inverse, cut))

    with jax.named_scope("all_rows"):
        pair = pl.pallas_call(
            pair_kernel,
            out_shape=jax.ShapeDtypeStruct((2, slot_rows, 2 * width), BF16),
            in_specs=[VMEM, VMEM, ANY],
            out_specs=VMEM,
        )(routed, rows_y, sent_rows)
        column = lax.axis_size("x")
        pairs = [pair] + [
            lax.ppermute(pair, "x", [(i, (i + s) % column) for i in range(column)])
            for s in range(1, column)
        ]

    with jax.named_scope("new_slices"):
        block = jax.ShapeDtypeStruct((chips, unit_width, width), BF16)
        up_part, down_part, their_up, their_down = pl.pallas_call(
            gradient_kernel,
            out_shape=(block,) * 4,
            in_specs=[VMEM] * 6 + [ANY],
            out_specs=(VMEM,) * 4,
            compiler_params=LARGE,
        )(own_units, other_units, *pairs, own_result)
        source = inverse // 2
        back = (lax.axis_index("x") - source % column) % column
        source = 2 * back + (source // column != lax.axis_index("y")).astype(jnp.int32)
        source = source + jnp.where(inverse % 2 == core, 0, chips)
        grad = jax.ShapeDtypeStruct((unit_width, cut_count * width), BF16)
        up_grad, down_grad = pl.pallas_call(
            layout_kernel,
            out_shape=(grad, grad),
            in_specs=[pl.BlockSpec(memory_space=pltpu.SMEM)] + [VMEM] * 4,
            out_specs=(VMEM, VMEM),
            compiler_params=LARGE,
        )(source, up_part, down_part, swap(their_up), swap(their_down))
    return (result[:, :width], result[:, width:], up_grad, down_grad)


def solution(mesh):
    experts, cuts = mesh.devices.shape
    split = Mesh(mesh.devices.reshape(experts, 2, cuts // 4, 2), ("expert", "y", "x", "core"))
    spread = P("expert", CUTS)
    return jax.shard_map(
        local,
        mesh=split,
        in_specs=(spread, P("expert", None), P("expert", None), spread, spread, P(), P(), spread),
        out_specs=(
            spread,
            spread,
            P(("expert", *CUTS), None),
            P(("expert", *CUTS), None),
        ),
        check_vma=False,
    )
```

```python
import jax
import jax.numpy as jnp
from jax import lax
from jax.experimental import pallas as pl
from jax.experimental.pallas import tpu as pltpu
from jax.sharding import Mesh, PartitionSpec as P

F32, BF16 = jnp.float32, jnp.bfloat16
CHIP = ("y", "x")
CUTS = ("y", "x", "core")
VMEM = pl.BlockSpec(memory_space=pltpu.VMEM)
ANY = pl.BlockSpec(memory_space=pl.ANY)
LARGE = pltpu.CompilerParams(vmem_limit_bytes=24 * 2**20)


def exchange(parts, axis):
    return lax.all_to_all(parts, axis, split_axis=0, concat_axis=0, tiled=True)


def everywhere(block, axis):
    return exchange(jnp.broadcast_to(block[None], (lax.axis_size(axis), *block.shape)), axis)


def swap(block):
    return lax.ppermute(block, "core", [(0, 1), (1, 0)])


def swap_y(block):
    return lax.ppermute(block, "y", [(0, 1), (1, 0)])


def pick(blocks, index):
    return lax.dynamic_index_in_dim(blocks, index, axis=0, keepdims=False)


def rows_at(blocks, places):
    return jnp.take(blocks, places, axis=0, mode="clip")


def pair_kernel(own_ref, x_ref, back_ref, after_ref, pair_ref, sems):
    width = x_ref.shape[1]
    copies = [
        pltpu.make_async_copy(own_ref, pair_ref.at[0], sems.at[0]),
        pltpu.make_async_copy(x_ref, pair_ref.at[1, :, pl.ds(0, width)], sems.at[1]),
        pltpu.make_async_copy(back_ref, pair_ref.at[1, :, pl.ds(width, width)], sems.at[2]),
    ]
    for copy in copies:
        copy.start()
    for copy in copies:
        copy.wait()


def gradient_kernel(own_units, other_units, first, second, after_ref, up_ref, down_ref, theirs_ref):
    unit_width, width = up_ref.shape[1:]
    hidden, pre_grad = [
        jnp.concatenate([own_units[part], other_units[part]], axis=0)
        for part in (pl.ds(0, unit_width), pl.ds(unit_width, unit_width))
    ]
    for j, rows in enumerate((first, second)):
        up = jnp.dot(pre_grad, rows[0, :, :width], preferred_element_type=F32).astype(BF16)
        down = jnp.dot(hidden, rows[0, :, width:], preferred_element_type=F32).astype(BF16)
        up_ref[j] = up[:unit_width]
        down_ref[j] = down[:unit_width]
        theirs_ref[j, :unit_width] = up[unit_width:]
        theirs_ref[j, unit_width:] = down[unit_width:]


def layout_kernel(source_ref, *refs):
    groups, (up_ref, down_ref) = (refs[:3], refs[3:6]), refs[6:]
    blocks, unit_width, width = refs[0].shape
    for p in range(4 * blocks):
        columns = pl.ds(p * width, width)
        source = source_ref[p]
        place = source % blocks
        for g, (own_up, own_down, theirs) in enumerate(groups):

            @pl.when(source // blocks == 2 * g)
            def _():
                up_ref[:, columns] = own_up[place]
                down_ref[:, columns] = own_down[place]

            @pl.when(source // blocks == 2 * g + 1)
            def _():
                up_ref[:, columns] = theirs[place, :unit_width]
                down_ref[:, columns] = theirs[place, unit_width:]


def local(tokens, expert_ids, gate_weights, old_up, old_down, old_rows, new_slots, cotangent):
    chips = lax.axis_size(CHIP)
    cut_count = 2 * chips
    group_count = lax.axis_size("expert")
    expert_count = group_count // 2
    tok_rows, width = tokens.shape
    half_units = old_up.shape[0]
    unit_width = half_units // cut_count
    core_units = half_units // 2
    capacity = 8 * tok_rows // group_count
    slot_rows = group_count * capacity
    chip, core = lax.axis_index(CHIP), lax.axis_index("core")
    cut = 2 * chip + core
    cut_list = jnp.arange(cut_count, dtype=jnp.int32)
    inverse = jnp.sum(
        cut_list[:, None] * (old_rows[:, None] == cut_list[None, :]).astype(jnp.int32), axis=0
    )
    slot_pairs = new_slots.reshape(chips, 2)
    kept, given = slot_pairs[:, core], slot_pairs[:, 1 - core]

    def both_blocks(weights):
        blocks = weights.reshape(cut_count, unit_width, width)
        mine, theirs = rows_at(blocks, kept), swap(rows_at(blocks, given))
        return jnp.concatenate([mine, theirs], axis=2).reshape(core_units, 2 * width)

    with jax.named_scope("weights"):
        up, down = both_blocks(old_up), both_blocks(old_down)

    with jax.named_scope("token_blocks"):
        both = everywhere(jnp.concatenate([tokens, cotangent], axis=1), CUTS)
        both = pick(both, pick(old_rows, cut))

    flat_ids = expert_ids.reshape(-1)
    expert_hits = (flat_ids[:, None] == jnp.arange(expert_count, dtype=jnp.int32)[None, :]).astype(
        jnp.int32
    )
    slot_rank = jnp.sum((jnp.cumsum(expert_hits, axis=0) - expert_hits) * expert_hits, axis=1)
    target = (flat_ids * capacity + slot_rank).reshape(tok_rows, 2)
    slots = expert_count * capacity
    slot_list = jnp.arange(slots, dtype=jnp.int32)
    matches = slot_list[:, None, None] == target[None]
    placer = jnp.any(matches, axis=2).astype(BF16)
    slot_gate = jnp.sum(jnp.where(matches, gate_weights[None], 0.0), axis=(1, 2))

    with jax.named_scope("dispatch"):
        placed = jnp.dot(placer, both, preferred_element_type=F32)
        scale = jnp.where(jnp.arange(2 * width)[None, :] < width, 1.0, slot_gate[:, None])
        placed = (placed * scale).astype(BF16).reshape(expert_count, 1, capacity, 2 * width)
        placed = jnp.broadcast_to(placed, (expert_count, 2, capacity, 2 * width))
        routed = exchange(placed.reshape(group_count, capacity, 2 * width), "expert")
        routed = routed.reshape(slot_rows, 2 * width)
        other = swap(routed)
        routed_x = jnp.concatenate([routed[:, :width], other[:, :width]], axis=1)
        routed_back = jnp.concatenate([routed[:, width:], other[:, width:]], axis=1)

    def partial(weights, rows):
        part = lax.dot_general(
            weights, rows, (((1,), (1,)), ((), ())), preferred_element_type=F32
        ).astype(BF16)
        return part.reshape(chips, unit_width, slot_rows)

    with jax.named_scope("hidden"):
        parts = jnp.concatenate([partial(up, routed_x), partial(down, routed_back)], axis=1)
        later_x, parts = lax.optimization_barrier((routed[:, :width], parts))
        x_y = swap_y(later_x)
        parts, x_y = lax.optimization_barrier((exchange(parts, CHIP), x_y))
        sums = jnp.sum(parts.astype(F32), axis=0)
        pre_act, hidden_grad = sums[:unit_width], sums[unit_width:]
        sig = jax.nn.sigmoid(pre_act)
        hidden = jax.nn.silu(pre_act).astype(BF16)
        pre_grad = (hidden_grad * sig * (1.0 + pre_act * (1.0 - sig))).astype(BF16)
        own_units = jnp.concatenate([hidden, pre_grad], axis=0)
        other_units = swap(own_units)
        later_back, own_units = lax.optimization_barrier((routed[:, width:], own_units))
        back_y = swap_y(later_back)
        units = everywhere(own_units, CHIP)
        units, back_y, other_units = lax.optimization_barrier((units, back_y, other_units))
        hidden = units[:, :unit_width].reshape(core_units, slot_rows)
        pre_grad = units[:, unit_width:].reshape(core_units, slot_rows)

    def rows_of(units, weights):
        return lax.dot_general(
            units, weights, (((0,), (0,)), ((), ())), preferred_element_type=F32
        )

    with jax.named_scope("give_back"):
        theirs = [rows_of(hidden, down[:, width:]), rows_of(pre_grad, up[:, width:])]
        theirs = swap(jnp.concatenate([part.astype(BF16) for part in theirs], axis=1))
        own = [rows_of(hidden, down[:, :width]), rows_of(pre_grad, up[:, :width])]
        half_rows = (jnp.concatenate(own, axis=1) + theirs.astype(F32)).astype(BF16)
        sent_rows = half_rows.reshape(group_count, capacity, 2 * width)
        half_rows = exchange(sent_rows, "expert")
        row_list = jnp.arange(slot_rows, dtype=jnp.int32)
        row_slot = row_list // (2 * capacity) * capacity + row_list % capacity
        picker = (target.reshape(-1)[:, None] == row_slot[None, :]).astype(BF16)
        entries = jnp.dot(picker, half_rows.reshape(slot_rows, 2 * width), preferred_element_type=F32)
        entries = entries.reshape(tok_rows, 2, 2 * width)
        mixed = jnp.sum(entries[:, :, :width] * gate_weights[:, :, None], axis=1)
        token_grad = jnp.sum(entries[:, :, width:], axis=1)
        result = jnp.concatenate([mixed, token_grad], axis=1).astype(BF16)

    with jax.named_scope("result"):
        own_result = result
        result = pick(everywhere(own_result, CUTS), pick(inverse, cut))

    with jax.named_scope("all_rows"):
        pair = pl.pallas_call(
            pair_kernel,
            out_shape=jax.ShapeDtypeStruct((2, slot_rows, 2 * width), BF16),
            in_specs=[ANY] * 4,
            out_specs=ANY,
            scratch_shapes=[pltpu.SemaphoreType.DMA((3,))],
        )(routed, x_y, back_y, sent_rows)
        column = lax.axis_size("x")
        pairs = [pair] + [
            lax.ppermute(pair, "x", [(i, (i + s) % column) for i in range(column)])
            for s in range(1, column)
        ]

    with jax.named_scope("new_slices"):
        units_spec = pl.BlockSpec((2 * unit_width, slot_rows), lambda t: (0, 0))
        rows_spec = pl.BlockSpec((1, slot_rows, 2 * width), lambda t: (t, 0, 0))
        part_spec = pl.BlockSpec((2, unit_width, width), lambda t: (t, 0, 0))
        part = jax.ShapeDtypeStruct((chips // 2, unit_width, width), BF16)
        held = []
        for g in range(2):
            up_part, down_part, theirs = pl.pallas_call(
                gradient_kernel,
                grid=(2,),
                out_shape=(
                    part,
                    part,
                    jax.ShapeDtypeStruct((chips // 2, 2 * unit_width, width), BF16),
                ),
                in_specs=[units_spec, units_spec, rows_spec, rows_spec, ANY],
                out_specs=(
                    part_spec,
                    part_spec,
                    pl.BlockSpec((2, 2 * unit_width, width), lambda t: (t, 0, 0)),
                ),
                compiler_params=LARGE,
            )(own_units, other_units, *pairs[2 * g : 2 * g + 2], own_result)
            held += [up_part, down_part, swap(theirs)]
        source = inverse // 2
        back = (lax.axis_index("x") - source % column) % column
        other_y = (source // column != lax.axis_index("y")).astype(jnp.int32)
        other_core = (inverse % 2 != core).astype(jnp.int32)
        source = 8 * (back // 2) + 4 * other_core + 2 * other_y + back % 2
        grad = jax.ShapeDtypeStruct((unit_width, cut_count * width), BF16)
        up_grad, down_grad = pl.pallas_call(
            layout_kernel,
            out_shape=(grad, grad),
            in_specs=[pl.BlockSpec(memory_space=pltpu.SMEM)] + [VMEM] * 6,
            out_specs=(VMEM, VMEM),
            compiler_params=LARGE,
        )(source, *held)
    return (result[:, :width], result[:, width:], up_grad, down_grad)


def solution(mesh):
    experts, cuts = mesh.devices.shape
    split = Mesh(mesh.devices.reshape(experts, 2, cuts // 4, 2), ("expert", "y", "x", "core"))
    spread = P("expert", CUTS)
    return jax.shard_map(
        local,
        mesh=split,
        in_specs=(spread, P("expert", None), P("expert", None), spread, spread, P(), P(), spread),
        out_specs=(
            spread,
            spread,
            P(("expert", *CUTS), None),
            P(("expert", *CUTS), None),
        ),
        check_vma=False,
    )
```

```python
import jax
import jax.numpy as jnp
from jax import lax
from jax.experimental import pallas as pl
from jax.experimental.pallas import tpu as pltpu
from jax.sharding import Mesh, PartitionSpec as P

F32, BF16 = jnp.float32, jnp.bfloat16
CHIP = ("y", "x")
CUTS = ("y", "x", "core")
VMEM = pl.BlockSpec(memory_space=pltpu.VMEM)
ANY = pl.BlockSpec(memory_space=pl.ANY)
LARGE = pltpu.CompilerParams(vmem_limit_bytes=24 * 2**20)


def exchange(parts, axis):
    return lax.all_to_all(parts, axis, split_axis=0, concat_axis=0, tiled=True)


def everywhere(block, axis):
    return exchange(jnp.broadcast_to(block[None], (lax.axis_size(axis), *block.shape)), axis)


def swap(block):
    return lax.ppermute(block, "core", [(0, 1), (1, 0)])


def pick(blocks, index):
    return lax.dynamic_index_in_dim(blocks, index, axis=0, keepdims=False)


def rows_at(blocks, places):
    return jnp.take(blocks, places, axis=0, mode="clip")


def gradient_kernel(own_units, other_units, first, second, after_ref, up_ref, down_ref, theirs_ref):
    unit_width, width = up_ref.shape[1:]
    hidden, pre_grad = [
        jnp.concatenate([own_units[part], other_units[part]], axis=0)
        for part in (pl.ds(0, unit_width), pl.ds(unit_width, unit_width))
    ]
    for j, rows in enumerate((first, second)):
        up = jnp.dot(pre_grad, rows[0, :, :width], preferred_element_type=F32).astype(BF16)
        down = jnp.dot(hidden, rows[0, :, width:], preferred_element_type=F32).astype(BF16)
        up_ref[j] = up[:unit_width]
        down_ref[j] = down[:unit_width]
        theirs_ref[j, :unit_width] = up[unit_width:]
        theirs_ref[j, unit_width:] = down[unit_width:]


def layout_kernel(source_ref, *refs):
    groups, (up_ref, down_ref) = (refs[:3], refs[3:6]), refs[6:]
    blocks, unit_width, width = refs[0].shape
    for p in range(4 * blocks):
        columns = pl.ds(p * width, width)
        source = source_ref[p]
        place = source % blocks
        for g, (own_up, own_down, theirs) in enumerate(groups):

            @pl.when(source // blocks == 2 * g)
            def _():
                up_ref[:, columns] = own_up[place]
                down_ref[:, columns] = own_down[place]

            @pl.when(source // blocks == 2 * g + 1)
            def _():
                up_ref[:, columns] = theirs[place, :unit_width]
                down_ref[:, columns] = theirs[place, unit_width:]


def local(tokens, expert_ids, gate_weights, old_up, old_down, old_rows, new_slots, cotangent):
    chips = lax.axis_size(CHIP)
    cut_count = 2 * chips
    group_count = lax.axis_size("expert")
    expert_count = group_count // 2
    tok_rows, width = tokens.shape
    half_units = old_up.shape[0]
    unit_width = half_units // cut_count
    core_units = half_units // 2
    capacity = 8 * tok_rows // group_count
    slot_rows = group_count * capacity
    chip, core = lax.axis_index(CHIP), lax.axis_index("core")
    cut = 2 * chip + core
    cut_list = jnp.arange(cut_count, dtype=jnp.int32)
    inverse = jnp.sum(
        cut_list[:, None] * (old_rows[:, None] == cut_list[None, :]).astype(jnp.int32), axis=0
    )
    slot_pairs = new_slots.reshape(chips, 2)
    kept, given = slot_pairs[:, core], slot_pairs[:, 1 - core]

    def both_blocks(weights):
        blocks = weights.reshape(cut_count, unit_width, width)
        mine, theirs = rows_at(blocks, kept), swap(rows_at(blocks, given))
        return jnp.concatenate([mine, theirs], axis=2).reshape(core_units, 2 * width)

    with jax.named_scope("weights"):
        up, down = both_blocks(old_up), both_blocks(old_down)

    with jax.named_scope("token_blocks"):
        both = everywhere(jnp.concatenate([tokens, cotangent], axis=1), CUTS)
        both = pick(both, pick(old_rows, cut))

    flat_ids = expert_ids.reshape(-1)
    expert_hits = (flat_ids[:, None] == jnp.arange(expert_count, dtype=jnp.int32)[None, :]).astype(
        jnp.int32
    )
    slot_rank = jnp.sum((jnp.cumsum(expert_hits, axis=0) - expert_hits) * expert_hits, axis=1)
    target = (flat_ids * capacity + slot_rank).reshape(tok_rows, 2)
    slots = expert_count * capacity
    slot_list = jnp.arange(slots, dtype=jnp.int32)
    matches = slot_list[:, None, None] == target[None]
    placer = jnp.any(matches, axis=2).astype(BF16)
    slot_gate = jnp.sum(jnp.where(matches, gate_weights[None], 0.0), axis=(1, 2))

    with jax.named_scope("dispatch"):
        placed = jnp.dot(placer, both, preferred_element_type=F32)
        scale = jnp.where(jnp.arange(2 * width)[None, :] < width, 1.0, slot_gate[:, None])
        placed = (placed * scale).astype(BF16).reshape(expert_count, 1, capacity, 2 * width)
        placed = jnp.broadcast_to(placed, (expert_count, 2, capacity, 2 * width))
        routed = exchange(placed.reshape(group_count, capacity, 2 * width), "expert")
        routed = routed.reshape(slot_rows, 2 * width)
        other = swap(routed)
        routed_x = jnp.concatenate([routed[:, :width], other[:, :width]], axis=1)
        routed_back = jnp.concatenate([routed[:, width:], other[:, width:]], axis=1)

    def partial(weights, rows):
        part = lax.dot_general(
            weights, rows, (((1,), (1,)), ((), ())), preferred_element_type=F32
        ).astype(BF16)
        return part.reshape(chips, unit_width, slot_rows)

    with jax.named_scope("hidden"):
        parts = jnp.concatenate([partial(up, routed_x), partial(down, routed_back)], axis=1)
        sums = jnp.sum(exchange(parts, CHIP).astype(F32), axis=0)
        pre_act, hidden_grad = sums[:unit_width], sums[unit_width:]
        sig = jax.nn.sigmoid(pre_act)
        hidden = jax.nn.silu(pre_act).astype(BF16)
        pre_grad = (hidden_grad * sig * (1.0 + pre_act * (1.0 - sig))).astype(BF16)
        own_units = jnp.concatenate([hidden, pre_grad], axis=0)
        other_units = swap(own_units)
        later_rows, own_units = lax.optimization_barrier((routed, own_units))
        rows_y = lax.ppermute(later_rows, "y", [(0, 1), (1, 0)])
        units = everywhere(own_units, CHIP)
        units, rows_y, other_units = lax.optimization_barrier((units, rows_y, other_units))
        hidden = units[:, :unit_width].reshape(core_units, slot_rows)
        pre_grad = units[:, unit_width:].reshape(core_units, slot_rows)

    def rows_of(units, weights):
        return lax.dot_general(
            units, weights, (((0,), (0,)), ((), ())), preferred_element_type=F32
        )

    with jax.named_scope("give_back"):
        theirs = [rows_of(hidden, down[:, width:]), rows_of(pre_grad, up[:, width:])]
        theirs = swap(jnp.concatenate([part.astype(BF16) for part in theirs], axis=1))
        own = [rows_of(hidden, down[:, :width]), rows_of(pre_grad, up[:, :width])]
        half_rows = (jnp.concatenate(own, axis=1) + theirs.astype(F32)).astype(BF16)
        sent_rows = half_rows.reshape(group_count, capacity, 2 * width)
        half_rows = exchange(sent_rows, "expert")
        row_list = jnp.arange(slot_rows, dtype=jnp.int32)
        row_slot = row_list // (2 * capacity) * capacity + row_list % capacity
        picker = (target.reshape(-1)[:, None] == row_slot[None, :]).astype(BF16)
        entries = jnp.dot(picker, half_rows.reshape(slot_rows, 2 * width), preferred_element_type=F32)
        entries = entries.reshape(tok_rows, 2, 2 * width)
        mixed = jnp.sum(entries[:, :, :width] * gate_weights[:, :, None], axis=1)
        token_grad = jnp.sum(entries[:, :, width:], axis=1)
        result = jnp.concatenate([mixed, token_grad], axis=1).astype(BF16)

    with jax.named_scope("result"):
        own_result = result
        result = pick(everywhere(own_result, CUTS), pick(inverse, cut))

    with jax.named_scope("all_rows"):
        pair = jnp.stack(lax.optimization_barrier((routed, rows_y, sent_rows))[:2])
        column = lax.axis_size("x")
        pairs = [pair] + [
            lax.ppermute(pair, "x", [(i, (i + s) % column) for i in range(column)])
            for s in range(1, column)
        ]

    with jax.named_scope("new_slices"):
        units_spec = pl.BlockSpec((2 * unit_width, slot_rows), lambda t: (0, 0))
        rows_spec = pl.BlockSpec((1, slot_rows, 2 * width), lambda t: (t, 0, 0))
        part_spec = pl.BlockSpec((2, unit_width, width), lambda t: (t, 0, 0))
        part = jax.ShapeDtypeStruct((chips // 2, unit_width, width), BF16)
        held = []
        for g in range(2):
            up_part, down_part, theirs = pl.pallas_call(
                gradient_kernel,
                grid=(2,),
                out_shape=(
                    part,
                    part,
                    jax.ShapeDtypeStruct((chips // 2, 2 * unit_width, width), BF16),
                ),
                in_specs=[units_spec, units_spec, rows_spec, rows_spec, ANY],
                out_specs=(
                    part_spec,
                    part_spec,
                    pl.BlockSpec((2, 2 * unit_width, width), lambda t: (t, 0, 0)),
                ),
                compiler_params=LARGE,
            )(own_units, other_units, *pairs[2 * g : 2 * g + 2], own_result)
            held += [up_part, down_part, swap(theirs)]
        source = inverse // 2
        back = (lax.axis_index("x") - source % column) % column
        other_y = (source // column != lax.axis_index("y")).astype(jnp.int32)
        other_core = (inverse % 2 != core).astype(jnp.int32)
        source = 8 * (back // 2) + 4 * other_core + 2 * other_y + back % 2
        grad = jax.ShapeDtypeStruct((unit_width, cut_count * width), BF16)
        up_grad, down_grad = pl.pallas_call(
            layout_kernel,
            out_shape=(grad, grad),
            in_specs=[pl.BlockSpec(memory_space=pltpu.SMEM)] + [VMEM] * 6,
            out_specs=(VMEM, VMEM),
            compiler_params=LARGE,
        )(source, *held)
    return (result[:, :width], result[:, width:], up_grad, down_grad)


def solution(mesh):
    experts, cuts = mesh.devices.shape
    split = Mesh(mesh.devices.reshape(experts, 2, cuts // 4, 2), ("expert", "y", "x", "core"))
    spread = P("expert", CUTS)
    return jax.shard_map(
        local,
        mesh=split,
        in_specs=(spread, P("expert", None), P("expert", None), spread, spread, P(), P(), spread),
        out_specs=(
            spread,
            spread,
            P(("expert", *CUTS), None),
            P(("expert", *CUTS), None),
        ),
        check_vma=False,
    )
```

```python
import jax
import jax.numpy as jnp
from jax import lax
from jax.experimental import pallas as pl
from jax.experimental.pallas import tpu as pltpu
from jax.sharding import Mesh, PartitionSpec as P

F32, BF16 = jnp.float32, jnp.bfloat16
CHIP = ("y", "x")
CUTS = ("y", "x", "core")
VMEM = pl.BlockSpec(memory_space=pltpu.VMEM)
ANY = pl.BlockSpec(memory_space=pl.ANY)
LARGE = pltpu.CompilerParams(vmem_limit_bytes=24 * 2**20)


def exchange(parts, axis):
    return lax.all_to_all(parts, axis, split_axis=0, concat_axis=0, tiled=True)


def everywhere(block, axis):
    return exchange(jnp.broadcast_to(block[None], (lax.axis_size(axis), *block.shape)), axis)


def swap(block):
    return lax.ppermute(block, "core", [(0, 1), (1, 0)])


def pick(blocks, index):
    return lax.dynamic_index_in_dim(blocks, index, axis=0, keepdims=False)


def rows_at(blocks, places):
    return jnp.take(blocks, places, axis=0, mode="clip")


def gradient_kernel(own_units, other_units, first, second, after_ref, up_ref, down_ref, theirs_ref):
    unit_width, width = up_ref.shape[1:]
    hidden, pre_grad = [
        jnp.concatenate([own_units[part], other_units[part]], axis=0)
        for part in (pl.ds(0, unit_width), pl.ds(unit_width, unit_width))
    ]
    for j, rows in enumerate((first, second)):
        up = jnp.dot(pre_grad, rows[0, :, :width], preferred_element_type=F32).astype(BF16)
        down = jnp.dot(hidden, rows[0, :, width:], preferred_element_type=F32).astype(BF16)
        up_ref[j] = up[:unit_width]
        down_ref[j] = down[:unit_width]
        theirs_ref[j, :unit_width] = up[unit_width:]
        theirs_ref[j, unit_width:] = down[unit_width:]


def layout_kernel(source_ref, *refs):
    groups, (up_ref, down_ref) = (refs[:3], refs[3:6]), refs[6:]
    blocks, unit_width, width = refs[0].shape
    for p in range(4 * blocks):
        columns = pl.ds(p * width, width)
        source = source_ref[p]
        place = source % blocks
        for g, (own_up, own_down, theirs) in enumerate(groups):

            @pl.when(source // blocks == 2 * g)
            def _():
                up_ref[:, columns] = own_up[place]
                down_ref[:, columns] = own_down[place]

            @pl.when(source // blocks == 2 * g + 1)
            def _():
                up_ref[:, columns] = theirs[place, :unit_width]
                down_ref[:, columns] = theirs[place, unit_width:]


def local(tokens, expert_ids, gate_weights, old_up, old_down, old_rows, new_slots, cotangent):
    chips = lax.axis_size(CHIP)
    cut_count = 2 * chips
    group_count = lax.axis_size("expert")
    expert_count = group_count // 2
    tok_rows, width = tokens.shape
    half_units = old_up.shape[0]
    unit_width = half_units // cut_count
    capacity = 8 * tok_rows // group_count
    slot_rows = group_count * capacity
    chip, core = lax.axis_index(CHIP), lax.axis_index("core")
    cut, other_cut = 2 * chip + core, 2 * chip + 1 - core
    cut_list = jnp.arange(cut_count, dtype=jnp.int32)
    inverse = jnp.sum(
        cut_list[:, None] * (old_rows[:, None] == cut_list[None, :]).astype(jnp.int32), axis=0
    )

    with jax.named_scope("weights"):
        shape = (chips, 2 * unit_width, width)
        up = [old_up.reshape(shape), swap(old_up).reshape(shape)]
        down = [old_down.reshape(shape), swap(old_down).reshape(shape)]

    with jax.named_scope("token_blocks"):
        blocks = everywhere(jnp.concatenate([tokens, cotangent], axis=1), CUTS)
        own, other = pick(blocks, pick(old_rows, cut)), pick(blocks, pick(old_rows, other_cut))
        both = jnp.concatenate(
            [own[:, :width], other[:, :width], own[:, width:], other[:, width:]], axis=1
        )

    flat_ids = expert_ids.reshape(-1)
    expert_hits = (flat_ids[:, None] == jnp.arange(expert_count, dtype=jnp.int32)[None, :]).astype(
        jnp.int32
    )
    slot_rank = jnp.sum((jnp.cumsum(expert_hits, axis=0) - expert_hits) * expert_hits, axis=1)
    target = (flat_ids * capacity + slot_rank).reshape(tok_rows, 2)
    held_slots = capacity // 2
    core_rows = slot_rows // 2
    slot_list = 2 * jnp.arange(expert_count * held_slots, dtype=jnp.int32) + core
    matches = slot_list[:, None, None] == target[None]
    placer = jnp.any(matches, axis=2).astype(BF16)
    slot_gate = jnp.sum(jnp.where(matches, gate_weights[None], 0.0), axis=(1, 2))

    with jax.named_scope("dispatch"):
        placed = jnp.dot(placer, both, preferred_element_type=F32)
        scale = jnp.where(jnp.arange(4 * width)[None, :] < 2 * width, 1.0, slot_gate[:, None])
        placed = (placed * scale).astype(BF16).reshape(expert_count, 1, held_slots, 4 * width)
        placed = jnp.broadcast_to(placed, (expert_count, 2, held_slots, 4 * width))
        rows = exchange(placed.reshape(group_count, held_slots, 4 * width), "expert")
        rows = rows.reshape(core_rows, 4 * width)

    def partial(weights, first):
        return sum(
            jnp.einsum(
                "rd,pud->pru",
                rows[:, first + j * width : first + (j + 1) * width],
                weights[j],
                preferred_element_type=F32,
            )
            for j in range(2)
        ).astype(BF16)

    with jax.named_scope("hidden"):
        parts = jnp.concatenate([partial(up, 0), partial(down, 2 * width)], axis=2)
        sums = jnp.sum(exchange(parts, CHIP).astype(F32), axis=0)
        pre_act, hidden_grad = sums[:, : 2 * unit_width], sums[:, 2 * unit_width :]
        sig = jax.nn.sigmoid(pre_act)
        hidden = jax.nn.silu(pre_act).astype(BF16)
        pre_grad = (hidden_grad * sig * (1.0 + pre_act * (1.0 - sig))).astype(BF16)
        own_units = jnp.concatenate([hidden, pre_grad], axis=1)

        others = swap(
            jnp.concatenate([rows[:, width : 2 * width], rows[:, 3 * width :]], axis=1)
        )
        routed = jnp.concatenate([rows[:, :width], rows[:, 2 * width : 3 * width]], axis=1)
        routed = jnp.concatenate([routed, others], axis=0)
        later_rows, own_units = lax.optimization_barrier((routed, own_units))
        rows_y = lax.ppermute(later_rows, "y", [(0, 1), (1, 0)])
        units = everywhere(own_units, CHIP)
        units, rows_y = lax.optimization_barrier((units, rows_y))
        hidden, pre_grad = units[:, :, : 2 * unit_width], units[:, :, 2 * unit_width :]

    def rows_of(units, weights):
        return jnp.einsum("pru,pud->rd", units, weights, preferred_element_type=F32).astype(BF16)

    with jax.named_scope("give_back"):
        half_rows = jnp.concatenate(
            [rows_of(part, weights[j]) for j in range(2) for part, weights in ((hidden, down), (pre_grad, up))],
            axis=1,
        )
        sent_rows = half_rows.reshape(group_count, held_slots, 4 * width)
        half_rows = exchange(sent_rows, "expert")
        row_list = jnp.arange(core_rows, dtype=jnp.int32)
        row_slot = row_list // capacity * capacity + row_list % held_slots * 2 + core
        picker = (target.reshape(-1)[:, None] == row_slot[None, :]).astype(BF16)
        entries = jnp.dot(picker, half_rows.reshape(core_rows, 4 * width), preferred_element_type=F32)
        is_out = jnp.arange(4 * width) // width % 2 == 0
        factor = jnp.where(is_out[None, None, :], gate_weights[:, :, None], 1.0)
        own_result = jnp.sum(entries.reshape(tok_rows, 2, 4 * width) * factor, axis=1).astype(BF16)

    with jax.named_scope("result"):
        got = everywhere(own_result, CHIP)

        def share(place):
            source = pick(inverse, place)
            first = jnp.where(source % 2 == core, 0, 2 * width)
            return lax.dynamic_slice(got, (source // 2, 0, first), (1, tok_rows, 2 * width))[0]

        result = (share(cut).astype(F32) + swap(share(other_cut)).astype(F32)).astype(BF16)

    with jax.named_scope("slot_units"):

        def of_slot(place):
            block = pick(new_slots, place)
            return [
                lax.dynamic_slice(
                    units, (block // 2, 0, first + block % 2 * unit_width), (1, core_rows, unit_width)
                )[0]
                for first in (0, 2 * unit_width)
            ]

        mine = of_slot(cut) + of_slot(other_cut)
        theirs = swap(jnp.concatenate(mine[2:] + mine[:2], axis=1))
        slot_units = jnp.concatenate([jnp.concatenate(mine, axis=1), theirs], axis=0).T
        own_units, other_units = slot_units[: 2 * unit_width], slot_units[2 * unit_width :]

    with jax.named_scope("all_rows"):
        pair = jnp.stack(lax.optimization_barrier((routed, rows_y, sent_rows))[:2])
        column = lax.axis_size("x")
        pairs = [pair] + [
            lax.ppermute(pair, "x", [(i, (i + s) % column) for i in range(column)])
            for s in range(1, column)
        ]

    with jax.named_scope("new_slices"):
        units_spec = pl.BlockSpec((2 * unit_width, slot_rows), lambda t: (0, 0))
        rows_spec = pl.BlockSpec((1, slot_rows, 2 * width), lambda t: (t, 0, 0))
        part_spec = pl.BlockSpec((2, unit_width, width), lambda t: (t, 0, 0))
        part = jax.ShapeDtypeStruct((chips // 2, unit_width, width), BF16)
        held = []
        for g in range(2):
            up_part, down_part, theirs = pl.pallas_call(
                gradient_kernel,
                grid=(2,),
                out_shape=(
                    part,
                    part,
                    jax.ShapeDtypeStruct((chips // 2, 2 * unit_width, width), BF16),
                ),
                in_specs=[units_spec, units_spec, rows_spec, rows_spec, ANY],
                out_specs=(
                    part_spec,
                    part_spec,
                    pl.BlockSpec((2, 2 * unit_width, width), lambda t: (t, 0, 0)),
                ),
                compiler_params=LARGE,
            )(own_units, other_units, *pairs[2 * g : 2 * g + 2], own_result)
            held += [up_part, down_part, swap(theirs)]
        source = inverse // 2
        back = (lax.axis_index("x") - source % column) % column
        other_y = (source // column != lax.axis_index("y")).astype(jnp.int32)
        other_core = (inverse % 2 != core).astype(jnp.int32)
        source = 8 * (back // 2) + 4 * other_core + 2 * other_y + back % 2
        grad = jax.ShapeDtypeStruct((unit_width, cut_count * width), BF16)
        up_grad, down_grad = pl.pallas_call(
            layout_kernel,
            out_shape=(grad, grad),
            in_specs=[pl.BlockSpec(memory_space=pltpu.SMEM)] + [VMEM] * 6,
            out_specs=(VMEM, VMEM),
            compiler_params=LARGE,
        )(source, *held)
    return (result[:, :width], result[:, width:], up_grad, down_grad)


def solution(mesh):
    experts, cuts = mesh.devices.shape
    split = Mesh(mesh.devices.reshape(experts, 2, cuts // 4, 2), ("expert", "y", "x", "core"))
    spread = P("expert", CUTS)
    return jax.shard_map(
        local,
        mesh=split,
        in_specs=(spread, P("expert", None), P("expert", None), spread, spread, P(), P(), spread),
        out_specs=(
            spread,
            spread,
            P(("expert", *CUTS), None),
            P(("expert", *CUTS), None),
        ),
        check_vma=False,
    )
```

```python
import jax
import jax.numpy as jnp
from jax import lax
from jax.experimental import pallas as pl
from jax.experimental.pallas import tpu as pltpu
from jax.sharding import Mesh, PartitionSpec as P

F32, BF16 = jnp.float32, jnp.bfloat16
CHIP = ("y", "x")
CUTS = ("y", "x", "core")
VMEM = pl.BlockSpec(memory_space=pltpu.VMEM)
ANY = pl.BlockSpec(memory_space=pl.ANY)
LARGE = pltpu.CompilerParams(vmem_limit_bytes=24 * 2**20)


def exchange(parts, axis):
    return lax.all_to_all(parts, axis, split_axis=0, concat_axis=0, tiled=True)


def everywhere(block, axis):
    return exchange(jnp.broadcast_to(block[None], (lax.axis_size(axis), *block.shape)), axis)


def swap(block):
    return lax.ppermute(block, "core", [(0, 1), (1, 0)])


def pick(blocks, index):
    return lax.dynamic_index_in_dim(blocks, index, axis=0, keepdims=False)


def rows_at(blocks, places):
    return jnp.take(blocks, places, axis=0, mode="clip")


def gradient_kernel(own_units, other_units, first, second, after_ref, up_ref, down_ref, theirs_ref):
    unit_width, width = up_ref.shape[1:]
    hidden, pre_grad = [
        jnp.concatenate([own_units[part], other_units[part]], axis=0)
        for part in (pl.ds(0, unit_width), pl.ds(unit_width, unit_width))
    ]
    for j, rows in enumerate((first, second)):
        up = jnp.dot(pre_grad, rows[0, :, :width], preferred_element_type=F32).astype(BF16)
        down = jnp.dot(hidden, rows[0, :, width:], preferred_element_type=F32).astype(BF16)
        up_ref[j] = up[:unit_width]
        down_ref[j] = down[:unit_width]
        theirs_ref[j, :unit_width] = up[unit_width:]
        theirs_ref[j, unit_width:] = down[unit_width:]


def layout_kernel(source_ref, *refs):
    groups, (up_ref, down_ref) = (refs[:3], refs[3:6]), refs[6:]
    blocks, unit_width, width = refs[0].shape
    for p in range(4 * blocks):
        columns = pl.ds(p * width, width)
        source = source_ref[p]
        place = source % blocks
        for g, (own_up, own_down, theirs) in enumerate(groups):

            @pl.when(source // blocks == 2 * g)
            def _():
                up_ref[:, columns] = own_up[place]
                down_ref[:, columns] = own_down[place]

            @pl.when(source // blocks == 2 * g + 1)
            def _():
                up_ref[:, columns] = theirs[place, :unit_width]
                down_ref[:, columns] = theirs[place, unit_width:]


def local(tokens, expert_ids, gate_weights, old_up, old_down, old_rows, new_slots, cotangent):
    chips = lax.axis_size(CHIP)
    cut_count = 2 * chips
    group_count = lax.axis_size("expert")
    expert_count = group_count // 2
    tok_rows, width = tokens.shape
    half_units = old_up.shape[0]
    unit_width = half_units // cut_count
    capacity = 8 * tok_rows // group_count
    slot_rows = group_count * capacity
    chip, core = lax.axis_index(CHIP), lax.axis_index("core")
    cut, other_cut = 2 * chip + core, 2 * chip + 1 - core
    cut_list = jnp.arange(cut_count, dtype=jnp.int32)
    inverse = jnp.sum(
        cut_list[:, None] * (old_rows[:, None] == cut_list[None, :]).astype(jnp.int32), axis=0
    )

    with jax.named_scope("weights"):
        shape = (chips, 2 * unit_width, width)
        up = [old_up.reshape(shape), swap(old_up).reshape(shape)]
        down = [old_down.reshape(shape), swap(old_down).reshape(shape)]

    with jax.named_scope("token_blocks"):
        blocks = everywhere(jnp.concatenate([tokens, cotangent], axis=1), CUTS)
        own, other = pick(blocks, pick(old_rows, cut)), pick(blocks, pick(old_rows, other_cut))
        both = jnp.concatenate(
            [own[:, :width], other[:, :width], own[:, width:], other[:, width:]], axis=1
        )

    flat_ids = expert_ids.reshape(-1)
    expert_hits = (flat_ids[:, None] == jnp.arange(expert_count, dtype=jnp.int32)[None, :]).astype(
        jnp.int32
    )
    slot_rank = jnp.sum((jnp.cumsum(expert_hits, axis=0) - expert_hits) * expert_hits, axis=1)
    target = (flat_ids * capacity + slot_rank).reshape(tok_rows, 2)
    held_slots = capacity // 2
    core_rows = slot_rows // 2
    slot_list = 2 * jnp.arange(expert_count * held_slots, dtype=jnp.int32) + core
    matches = slot_list[:, None, None] == target[None]
    placer = jnp.any(matches, axis=2).astype(BF16)
    slot_gate = jnp.sum(jnp.where(matches, gate_weights[None], 0.0), axis=(1, 2))

    with jax.named_scope("dispatch"):
        placed = jnp.dot(placer, both, preferred_element_type=F32)
        scale = jnp.where(jnp.arange(4 * width)[None, :] < 2 * width, 1.0, slot_gate[:, None])
        placed = (placed * scale).astype(BF16).reshape(expert_count, 1, held_slots, 4 * width)
        placed = jnp.broadcast_to(placed, (expert_count, 2, held_slots, 4 * width))
        rows = exchange(placed.reshape(group_count, held_slots, 4 * width), "expert")
        rows = rows.reshape(core_rows, 4 * width)

    def found(place):
        source = pick(inverse, place)
        return source // 2, jnp.where(source % 2 == core, 0, 2 * width)

    def slot(place):
        block = pick(new_slots, place)
        return block // 2, block % 2 * unit_width

    column = lax.axis_size("x")
    source = inverse // 2
    back = (lax.axis_index("x") - source % column) % column
    other_y = (source // column != lax.axis_index("y")).astype(jnp.int32)
    other_core = (inverse % 2 != core).astype(jnp.int32)
    source = 8 * (back // 2) + 4 * other_core + 2 * other_y + back % 2
    row_list = jnp.arange(core_rows, dtype=jnp.int32)
    row_slot = row_list // capacity * capacity + row_list % held_slots * 2 + core
    picker = (target.reshape(-1)[:, None] == row_slot[None, :]).astype(BF16)
    places = [*found(cut), *found(other_cut), *slot(cut), *slot(other_cut)]
    rows, source, picker, places = lax.optimization_barrier((rows, source, picker, places))

    def partial(weights, first):
        return sum(
            jnp.einsum(
                "rd,pud->pru",
                rows[:, first + j * width : first + (j + 1) * width],
                weights[j],
                preferred_element_type=F32,
            )
            for j in range(2)
        ).astype(BF16)

    with jax.named_scope("hidden"):
        parts = jnp.concatenate([partial(up, 0), partial(down, 2 * width)], axis=2)
        sums = jnp.sum(exchange(parts, CHIP).astype(F32), axis=0)
        pre_act, hidden_grad = sums[:, : 2 * unit_width], sums[:, 2 * unit_width :]
        sig = jax.nn.sigmoid(pre_act)
        hidden = jax.nn.silu(pre_act).astype(BF16)
        pre_grad = (hidden_grad * sig * (1.0 + pre_act * (1.0 - sig))).astype(BF16)
        own_units = jnp.concatenate([hidden, pre_grad], axis=1)

        others = swap(
            jnp.concatenate([rows[:, width : 2 * width], rows[:, 3 * width :]], axis=1)
        )
        routed = jnp.concatenate([rows[:, :width], rows[:, 2 * width : 3 * width]], axis=1)
        routed = jnp.concatenate([routed, others], axis=0)
        later_rows, own_units = lax.optimization_barrier((routed, own_units))
        rows_y = lax.ppermute(later_rows, "y", [(0, 1), (1, 0)])
        units = everywhere(own_units, CHIP)
        units, rows_y = lax.optimization_barrier((units, rows_y))
        hidden, pre_grad = units[:, :, : 2 * unit_width], units[:, :, 2 * unit_width :]

    def rows_of(units, weights):
        return jnp.einsum("pru,pud->rd", units, weights, preferred_element_type=F32).astype(BF16)

    with jax.named_scope("give_back"):
        half_rows = jnp.concatenate(
            [rows_of(part, weights[j]) for j in range(2) for part, weights in ((hidden, down), (pre_grad, up))],
            axis=1,
        )
        sent_rows = half_rows.reshape(group_count, held_slots, 4 * width)
        half_rows = exchange(sent_rows, "expert")
        entries = jnp.dot(picker, half_rows.reshape(core_rows, 4 * width), preferred_element_type=F32)
        is_out = jnp.arange(4 * width) // width % 2 == 0
        factor = jnp.where(is_out[None, None, :], gate_weights[:, :, None], 1.0)
        own_result = jnp.sum(entries.reshape(tok_rows, 2, 4 * width) * factor, axis=1).astype(BF16)

    with jax.named_scope("result"):
        got = everywhere(own_result, CHIP)

        def share(chip_from, first):
            return lax.dynamic_slice(got, (chip_from, 0, first), (1, tok_rows, 2 * width))[0]

        own_share, their_share = share(*places[0:2]), swap(share(*places[2:4]))

    with jax.named_scope("slot_units"):

        def of_slot(chip_from, first):
            size = (1, core_rows, unit_width)
            return [
                lax.dynamic_slice(units, (chip_from, 0, first + part), size)[0]
                for part in (0, 2 * unit_width)
            ]

        mine = of_slot(*places[4:6]) + of_slot(*places[6:8])
        theirs = swap(jnp.concatenate(mine[2:] + mine[:2], axis=1))
        slot_units = jnp.concatenate([jnp.concatenate(mine, axis=1), theirs], axis=0).T
        own_units, other_units = slot_units[: 2 * unit_width], slot_units[2 * unit_width :]

    with jax.named_scope("all_rows"):
        pair = jnp.stack(lax.optimization_barrier((routed, rows_y, sent_rows))[:2])
        pairs = [pair] + [
            lax.ppermute(pair, "x", [(i, (i + s) % column) for i in range(column)])
            for s in range(1, column)
        ]

    with jax.named_scope("new_slices"):
        units_spec = pl.BlockSpec((2 * unit_width, slot_rows), lambda t: (0, 0))
        rows_spec = pl.BlockSpec((1, slot_rows, 2 * width), lambda t: (t, 0, 0))
        part_spec = pl.BlockSpec((2, unit_width, width), lambda t: (t, 0, 0))
        part = jax.ShapeDtypeStruct((chips // 2, unit_width, width), BF16)
        held = []
        for g in range(2):
            up_part, down_part, theirs = pl.pallas_call(
                gradient_kernel,
                grid=(2,),
                out_shape=(
                    part,
                    part,
                    jax.ShapeDtypeStruct((chips // 2, 2 * unit_width, width), BF16),
                ),
                in_specs=[units_spec, units_spec, rows_spec, rows_spec, ANY],
                out_specs=(
                    part_spec,
                    part_spec,
                    pl.BlockSpec((2, 2 * unit_width, width), lambda t: (t, 0, 0)),
                ),
                compiler_params=LARGE,
            )(own_units, other_units, *pairs[2 * g : 2 * g + 2], own_result)
            held += [up_part, down_part, swap(theirs)]
        grad = jax.ShapeDtypeStruct((unit_width, cut_count * width), BF16)
        up_grad, down_grad = pl.pallas_call(
            layout_kernel,
            out_shape=(grad, grad),
            in_specs=[pl.BlockSpec(memory_space=pltpu.SMEM)] + [VMEM] * 6,
            out_specs=(VMEM, VMEM),
            compiler_params=LARGE,
        )(source, *held)
        their_share, up_grad, down_grad = lax.optimization_barrier(
            (their_share, up_grad, down_grad)
        )
    result = (own_share.astype(F32) + their_share.astype(F32)).astype(BF16)
    return (result[:, :width], result[:, width:], up_grad, down_grad)


def solution(mesh):
    experts, cuts = mesh.devices.shape
    split = Mesh(mesh.devices.reshape(experts, 2, cuts // 4, 2), ("expert", "y", "x", "core"))
    spread = P("expert", CUTS)
    return jax.shard_map(
        local,
        mesh=split,
        in_specs=(spread, P("expert", None), P("expert", None), spread, spread, P(), P(), spread),
        out_specs=(
            spread,
            spread,
            P(("expert", *CUTS), None),
            P(("expert", *CUTS), None),
        ),
        check_vma=False,
    )
```

```python
import jax
import jax.numpy as jnp
from jax import lax
from jax.experimental import pallas as pl
from jax.experimental.pallas import tpu as pltpu
from jax.sharding import Mesh, PartitionSpec as P

F32, BF16 = jnp.float32, jnp.bfloat16
CHIP = ("y", "x")
CUTS = ("y", "x", "core")
VMEM = pl.BlockSpec(memory_space=pltpu.VMEM)
ANY = pl.BlockSpec(memory_space=pl.ANY)
LARGE = pltpu.CompilerParams(vmem_limit_bytes=24 * 2**20)


def exchange(parts, axis):
    return lax.all_to_all(parts, axis, split_axis=0, concat_axis=0, tiled=True)


def everywhere(block, axis):
    return exchange(jnp.broadcast_to(block[None], (lax.axis_size(axis), *block.shape)), axis)


def swap(block):
    return lax.ppermute(block, "core", [(0, 1), (1, 0)])


def pick(blocks, index):
    return lax.dynamic_index_in_dim(blocks, index, axis=0, keepdims=False)


def rows_at(blocks, places):
    return jnp.take(blocks, places, axis=0, mode="clip")


def gradient_kernel(own_units, other_units, first, second, after_ref, up_ref, down_ref, theirs_ref):
    unit_width, width = up_ref.shape[1:]
    hidden, pre_grad = [
        jnp.concatenate([own_units[part], other_units[part]], axis=0)
        for part in (pl.ds(0, unit_width), pl.ds(unit_width, unit_width))
    ]
    for j, rows in enumerate((first, second)):
        up = jnp.dot(pre_grad, rows[0, :, :width], preferred_element_type=F32).astype(BF16)
        down = jnp.dot(hidden, rows[0, :, width:], preferred_element_type=F32).astype(BF16)
        up_ref[j] = up[:unit_width]
        down_ref[j] = down[:unit_width]
        theirs_ref[j, :unit_width] = up[unit_width:]
        theirs_ref[j, unit_width:] = down[unit_width:]


def layout_kernel(source_ref, *refs):
    groups, (up_ref, down_ref) = (refs[:3], refs[3:6]), refs[6:]
    blocks, unit_width, width = refs[0].shape
    for p in range(4 * blocks):
        columns = pl.ds(p * width, width)
        source = source_ref[p]
        place = source % blocks
        for g, (own_up, own_down, theirs) in enumerate(groups):

            @pl.when(source // blocks == 2 * g)
            def _():
                up_ref[:, columns] = own_up[place]
                down_ref[:, columns] = own_down[place]

            @pl.when(source // blocks == 2 * g + 1)
            def _():
                up_ref[:, columns] = theirs[place, :unit_width]
                down_ref[:, columns] = theirs[place, unit_width:]


def local(tokens, expert_ids, gate_weights, old_up, old_down, old_rows, new_slots, cotangent):
    chips = lax.axis_size(CHIP)
    cut_count = 2 * chips
    group_count = lax.axis_size("expert")
    expert_count = group_count // 2
    tok_rows, width = tokens.shape
    half_units = old_up.shape[0]
    unit_width = half_units // cut_count
    capacity = 8 * tok_rows // group_count
    slot_rows = group_count * capacity
    chip, core = lax.axis_index(CHIP), lax.axis_index("core")
    cut, other_cut = 2 * chip + core, 2 * chip + 1 - core
    cut_list = jnp.arange(cut_count, dtype=jnp.int32)
    inverse = jnp.sum(
        cut_list[:, None] * (old_rows[:, None] == cut_list[None, :]).astype(jnp.int32), axis=0
    )

    def in_slots(weights):
        blocks = rows_at(weights.reshape(cut_count, unit_width, width), new_slots)
        shape = (chips, 2 * unit_width, width)
        return [blocks.reshape(shape), swap(blocks).reshape(shape)]

    with jax.named_scope("weights"):
        up, down = in_slots(old_up), in_slots(old_down)

    with jax.named_scope("token_blocks"):
        blocks = everywhere(jnp.concatenate([tokens, cotangent], axis=1), CUTS)
        own, other = pick(blocks, pick(old_rows, cut)), pick(blocks, pick(old_rows, other_cut))
        both = jnp.concatenate(
            [own[:, :width], other[:, :width], own[:, width:], other[:, width:]], axis=1
        )

    flat_ids = expert_ids.reshape(-1)
    expert_hits = (flat_ids[:, None] == jnp.arange(expert_count, dtype=jnp.int32)[None, :]).astype(
        jnp.int32
    )
    slot_rank = jnp.sum((jnp.cumsum(expert_hits, axis=0) - expert_hits) * expert_hits, axis=1)
    target = (flat_ids * capacity + slot_rank).reshape(tok_rows, 2)
    held_slots = capacity // 2
    core_rows = slot_rows // 2
    slot_list = 2 * jnp.arange(expert_count * held_slots, dtype=jnp.int32) + core
    matches = slot_list[:, None, None] == target[None]
    placer = jnp.any(matches, axis=2).astype(BF16)
    slot_gate = jnp.sum(jnp.where(matches, gate_weights[None], 0.0), axis=(1, 2))

    with jax.named_scope("dispatch"):
        placed = jnp.dot(placer, both, preferred_element_type=F32)
        scale = jnp.where(jnp.arange(4 * width)[None, :] < 2 * width, 1.0, slot_gate[:, None])
        placed = (placed * scale).astype(BF16).reshape(expert_count, 1, held_slots, 4 * width)
        placed = jnp.broadcast_to(placed, (expert_count, 2, held_slots, 4 * width))
        rows = exchange(placed.reshape(group_count, held_slots, 4 * width), "expert")
        rows = rows.reshape(core_rows, 4 * width)

    def found(place):
        source = pick(inverse, place)
        return source // 2, jnp.where(source % 2 == core, 0, 2 * width)

    column = lax.axis_size("x")
    source = inverse // 2
    back = (lax.axis_index("x") - source % column) % column
    other_y = (source // column != lax.axis_index("y")).astype(jnp.int32)
    other_core = (inverse % 2 != core).astype(jnp.int32)
    source = 8 * (back // 2) + 4 * other_core + 2 * other_y + back % 2
    row_list = jnp.arange(core_rows, dtype=jnp.int32)
    row_slot = row_list // capacity * capacity + row_list % held_slots * 2 + core
    picker = (target.reshape(-1)[:, None] == row_slot[None, :]).astype(BF16)
    places = [*found(cut), *found(other_cut)]
    rows, source, picker, places = lax.optimization_barrier((rows, source, picker, places))

    def partial(weights, first):
        return sum(
            jnp.einsum(
                "rd,pud->pru",
                rows[:, first + j * width : first + (j + 1) * width],
                weights[j],
                preferred_element_type=F32,
            )
            for j in range(2)
        ).astype(BF16)

    with jax.named_scope("hidden"):
        parts = jnp.concatenate([partial(up, 0), partial(down, 2 * width)], axis=2)
        sums = jnp.sum(exchange(parts, CHIP).astype(F32), axis=0)
        pre_act, hidden_grad = sums[:, : 2 * unit_width], sums[:, 2 * unit_width :]
        sig = jax.nn.sigmoid(pre_act)
        hidden = jax.nn.silu(pre_act).astype(BF16)
        pre_grad = (hidden_grad * sig * (1.0 + pre_act * (1.0 - sig))).astype(BF16)
        own_units = jnp.concatenate([hidden, pre_grad], axis=1)

        others = swap(
            jnp.concatenate([rows[:, width : 2 * width], rows[:, 3 * width :]], axis=1)
        )
        routed = jnp.concatenate([rows[:, :width], rows[:, 2 * width : 3 * width]], axis=1)
        routed = jnp.concatenate([routed, others], axis=0)
        later_rows, own_units = lax.optimization_barrier((routed, own_units))
        rows_y = lax.ppermute(later_rows, "y", [(0, 1), (1, 0)])
        halves = [own_units[:, i * unit_width : (i + 1) * unit_width] for i in range(4)]
        mine = [jnp.where(core == 0, halves[i], halves[i + 1]) for i in (0, 2)]
        mine += [jnp.where(core == 0, halves[i + 1], halves[i]) for i in (0, 2)]
        theirs = swap(jnp.concatenate(mine[2:] + mine[:2], axis=1))
        slot_units = jnp.concatenate([jnp.concatenate(mine, axis=1), theirs], axis=0).T
        units = everywhere(own_units, CHIP)
        units, rows_y, slot_units = lax.optimization_barrier((units, rows_y, slot_units))
        hidden, pre_grad = units[:, :, : 2 * unit_width], units[:, :, 2 * unit_width :]

    def rows_of(units, weights):
        return jnp.einsum("pru,pud->rd", units, weights, preferred_element_type=F32).astype(BF16)

    with jax.named_scope("give_back"):
        half_rows = jnp.concatenate(
            [rows_of(part, weights[j]) for j in range(2) for part, weights in ((hidden, down), (pre_grad, up))],
            axis=1,
        )
        sent_rows = half_rows.reshape(group_count, held_slots, 4 * width)
        half_rows = exchange(sent_rows, "expert")
        entries = jnp.dot(picker, half_rows.reshape(core_rows, 4 * width), preferred_element_type=F32)
        is_out = jnp.arange(4 * width) // width % 2 == 0
        factor = jnp.where(is_out[None, None, :], gate_weights[:, :, None], 1.0)
        own_result = jnp.sum(entries.reshape(tok_rows, 2, 4 * width) * factor, axis=1).astype(BF16)

    with jax.named_scope("result"):
        got = everywhere(own_result, CHIP)

        def share(chip_from, first):
            return lax.dynamic_slice(got, (chip_from, 0, first), (1, tok_rows, 2 * width))[0]

        own_share, their_share = share(*places[0:2]), swap(share(*places[2:4]))

    with jax.named_scope("all_rows"):
        pair = jnp.stack(lax.optimization_barrier((routed, rows_y, sent_rows))[:2])
        pairs = [pair] + [
            lax.ppermute(pair, "x", [(i, (i + s) % column) for i in range(column)])
            for s in range(1, column)
        ]

    with jax.named_scope("new_slices"):
        own_units, other_units = slot_units[: 2 * unit_width], slot_units[2 * unit_width :]
        units_spec = pl.BlockSpec((2 * unit_width, slot_rows), lambda t: (0, 0))
        rows_spec = pl.BlockSpec((1, slot_rows, 2 * width), lambda t: (t, 0, 0))
        part_spec = pl.BlockSpec((2, unit_width, width), lambda t: (t, 0, 0))
        part = jax.ShapeDtypeStruct((chips // 2, unit_width, width), BF16)
        held = []
        for g in range(2):
            up_part, down_part, theirs = pl.pallas_call(
                gradient_kernel,
                grid=(2,),
                out_shape=(
                    part,
                    part,
                    jax.ShapeDtypeStruct((chips // 2, 2 * unit_width, width), BF16),
                ),
                in_specs=[units_spec, units_spec, rows_spec, rows_spec, ANY],
                out_specs=(
                    part_spec,
                    part_spec,
                    pl.BlockSpec((2, 2 * unit_width, width), lambda t: (t, 0, 0)),
                ),
                compiler_params=LARGE,
            )(own_units, other_units, *pairs[2 * g : 2 * g + 2], own_result)
            held += [up_part, down_part, swap(theirs)]
        grad = jax.ShapeDtypeStruct((unit_width, cut_count * width), BF16)
        up_grad, down_grad = pl.pallas_call(
            layout_kernel,
            out_shape=(grad, grad),
            in_specs=[pl.BlockSpec(memory_space=pltpu.SMEM)] + [VMEM] * 6,
            out_specs=(VMEM, VMEM),
            compiler_params=LARGE,
        )(source, *held)
        their_share, up_grad, down_grad = lax.optimization_barrier(
            (their_share, up_grad, down_grad)
        )
    result = (own_share.astype(F32) + their_share.astype(F32)).astype(BF16)
    return (result[:, :width], result[:, width:], up_grad, down_grad)


def solution(mesh):
    experts, cuts = mesh.devices.shape
    split = Mesh(mesh.devices.reshape(experts, 2, cuts // 4, 2), ("expert", "y", "x", "core"))
    spread = P("expert", CUTS)
    return jax.shard_map(
        local,
        mesh=split,
        in_specs=(spread, P("expert", None), P("expert", None), spread, spread, P(), P(), spread),
        out_specs=(
            spread,
            spread,
            P(("expert", *CUTS), None),
            P(("expert", *CUTS), None),
        ),
        check_vma=False,
    )
```

```python
import jax
import jax.numpy as jnp
from jax import lax
from jax.experimental import pallas as pl
from jax.experimental.pallas import tpu as pltpu
from jax.sharding import Mesh, PartitionSpec as P

F32, BF16 = jnp.float32, jnp.bfloat16
CHIP = ("y", "x")
CUTS = ("y", "x", "core")
VMEM = pl.BlockSpec(memory_space=pltpu.VMEM)
ANY = pl.BlockSpec(memory_space=pl.ANY)
LARGE = pltpu.CompilerParams(vmem_limit_bytes=8 * 2**20)


def exchange(parts, axis):
    return lax.all_to_all(parts, axis, split_axis=0, concat_axis=0, tiled=True)


def everywhere(block, axis):
    return exchange(jnp.broadcast_to(block[None], (lax.axis_size(axis), *block.shape)), axis)


def swap(block):
    return lax.ppermute(block, "core", [(0, 1), (1, 0)])


def pick(blocks, index):
    return lax.dynamic_index_in_dim(blocks, index, axis=0, keepdims=False)


def rows_at(blocks, places):
    return jnp.take(blocks, places, axis=0, mode="clip")


def gradient_kernel(own_units, other_units, first, second, after_ref, up_ref, down_ref, theirs_ref):
    unit_width, width = up_ref.shape[1:]
    hidden, pre_grad = [
        jnp.concatenate([own_units[part], other_units[part]], axis=0)
        for part in (pl.ds(0, unit_width), pl.ds(unit_width, unit_width))
    ]
    for j, rows in enumerate((first, second)):
        up = jnp.dot(pre_grad, rows[0, :, :width], preferred_element_type=F32).astype(BF16)
        down = jnp.dot(hidden, rows[0, :, width:], preferred_element_type=F32).astype(BF16)
        up_ref[j] = up[:unit_width]
        down_ref[j] = down[:unit_width]
        theirs_ref[j, :unit_width] = up[unit_width:]
        theirs_ref[j, unit_width:] = down[unit_width:]


def layout_kernel(source_ref, *refs):
    groups, (up_ref, down_ref) = (refs[:3], refs[3:6]), refs[6:]
    blocks, unit_width, width = refs[0].shape
    for p in range(4 * blocks):
        columns = pl.ds(p * width, width)
        source = source_ref[p]
        place = source % blocks
        for g, (own_up, own_down, theirs) in enumerate(groups):

            @pl.when(source // blocks == 2 * g)
            def _():
                up_ref[:, columns] = own_up[place]
                down_ref[:, columns] = own_down[place]

            @pl.when(source // blocks == 2 * g + 1)
            def _():
                up_ref[:, columns] = theirs[place, :unit_width]
                down_ref[:, columns] = theirs[place, unit_width:]


def local(tokens, expert_ids, gate_weights, old_up, old_down, old_rows, new_slots, cotangent):
    chips = lax.axis_size(CHIP)
    cut_count = 2 * chips
    group_count = lax.axis_size("expert")
    expert_count = group_count // 2
    tok_rows, width = tokens.shape
    half_units = old_up.shape[0]
    unit_width = half_units // cut_count
    capacity = 8 * tok_rows // group_count
    slot_rows = group_count * capacity
    chip, core = lax.axis_index(CHIP), lax.axis_index("core")
    cut, other_cut = 2 * chip + core, 2 * chip + 1 - core
    cut_list = jnp.arange(cut_count, dtype=jnp.int32)
    inverse = jnp.sum(
        cut_list[:, None] * (old_rows[:, None] == cut_list[None, :]).astype(jnp.int32), axis=0
    )

    with jax.named_scope("weights"):
        shape = (chips, 2 * unit_width, width)
        up = [old_up.reshape(shape), swap(old_up).reshape(shape)]
        down = [old_down.reshape(shape), swap(old_down).reshape(shape)]

    with jax.named_scope("token_blocks"):
        blocks = everywhere(jnp.concatenate([tokens, cotangent], axis=1), CUTS)
        own, other = pick(blocks, pick(old_rows, cut)), pick(blocks, pick(old_rows, other_cut))
        both = jnp.concatenate(
            [own[:, :width], other[:, :width], own[:, width:], other[:, width:]], axis=1
        )

    flat_ids = expert_ids.reshape(-1)
    expert_hits = (flat_ids[:, None] == jnp.arange(expert_count, dtype=jnp.int32)[None, :]).astype(
        jnp.int32
    )
    slot_rank = jnp.sum((jnp.cumsum(expert_hits, axis=0) - expert_hits) * expert_hits, axis=1)
    target = (flat_ids * capacity + slot_rank).reshape(tok_rows, 2)
    held_slots = capacity // 2
    core_rows = slot_rows // 2
    slot_list = 2 * jnp.arange(expert_count * held_slots, dtype=jnp.int32) + core
    matches = slot_list[:, None, None] == target[None]
    placer = jnp.any(matches, axis=2).astype(BF16)
    slot_gate = jnp.sum(jnp.where(matches, gate_weights[None], 0.0), axis=(1, 2))

    with jax.named_scope("dispatch"):
        placed = jnp.dot(placer, both, preferred_element_type=F32)
        scale = jnp.where(jnp.arange(4 * width)[None, :] < 2 * width, 1.0, slot_gate[:, None])
        placed = (placed * scale).astype(BF16).reshape(expert_count, 1, held_slots, 4 * width)
        placed = jnp.broadcast_to(placed, (expert_count, 2, held_slots, 4 * width))
        rows = exchange(placed.reshape(group_count, held_slots, 4 * width), "expert")
        rows = rows.reshape(core_rows, 4 * width)

    def found(place):
        source = pick(inverse, place)
        return source // 2, jnp.where(source % 2 == core, 0, 2 * width)

    def slot(place):
        block = pick(new_slots, place)
        return block // 2, block % 2 * unit_width

    column = lax.axis_size("x")
    source = inverse // 2
    back = (lax.axis_index("x") - source % column) % column
    other_y = (source // column != lax.axis_index("y")).astype(jnp.int32)
    other_core = (inverse % 2 != core).astype(jnp.int32)
    source = 8 * (back // 2) + 4 * other_core + 2 * other_y + back % 2
    row_list = jnp.arange(core_rows, dtype=jnp.int32)
    row_slot = row_list // capacity * capacity + row_list % held_slots * 2 + core
    picker = (target.reshape(-1)[:, None] == row_slot[None, :]).astype(BF16)
    places = [*found(cut), *found(other_cut), *slot(cut), *slot(other_cut)]
    rows, source, picker, places = lax.optimization_barrier((rows, source, picker, places))

    def partial(weights, first):
        return sum(
            jnp.einsum(
                "rd,pud->pru",
                rows[:, first + j * width : first + (j + 1) * width],
                weights[j],
                preferred_element_type=F32,
            )
            for j in range(2)
        ).astype(BF16)

    with jax.named_scope("hidden"):
        parts = jnp.concatenate([partial(up, 0), partial(down, 2 * width)], axis=2)
        sums = jnp.sum(exchange(parts, CHIP).astype(F32), axis=0)
        pre_act, hidden_grad = sums[:, : 2 * unit_width], sums[:, 2 * unit_width :]
        sig = jax.nn.sigmoid(pre_act)
        hidden = jax.nn.silu(pre_act).astype(BF16)
        pre_grad = (hidden_grad * sig * (1.0 + pre_act * (1.0 - sig))).astype(BF16)
        own_units = jnp.concatenate([hidden, pre_grad], axis=1)

        others = swap(
            jnp.concatenate([rows[:, width : 2 * width], rows[:, 3 * width :]], axis=1)
        )
        routed = jnp.concatenate([rows[:, :width], rows[:, 2 * width : 3 * width]], axis=1)
        routed = jnp.concatenate([routed, others], axis=0)
        later_rows, own_units = lax.optimization_barrier((routed, own_units))
        rows_y = lax.ppermute(later_rows, "y", [(0, 1), (1, 0)])
        units = everywhere(own_units, CHIP)
        units, rows_y = lax.optimization_barrier((units, rows_y))
        hidden, pre_grad = units[:, :, : 2 * unit_width], units[:, :, 2 * unit_width :]

    def rows_of(units, weights):
        return jnp.einsum("pru,pud->rd", units, weights, preferred_element_type=F32).astype(BF16)

    with jax.named_scope("give_back"):
        half_rows = jnp.concatenate(
            [rows_of(part, weights[j]) for j in range(2) for part, weights in ((hidden, down), (pre_grad, up))],
            axis=1,
        )
        sent_rows = half_rows.reshape(group_count, held_slots, 4 * width)
        half_rows = exchange(sent_rows, "expert")
        entries = jnp.dot(picker, half_rows.reshape(core_rows, 4 * width), preferred_element_type=F32)
        is_out = jnp.arange(4 * width) // width % 2 == 0
        factor = jnp.where(is_out[None, None, :], gate_weights[:, :, None], 1.0)
        own_result = jnp.sum(entries.reshape(tok_rows, 2, 4 * width) * factor, axis=1).astype(BF16)

    with jax.named_scope("result"):
        got = everywhere(own_result, CHIP)

        def share(chip_from, first):
            return lax.dynamic_slice(got, (chip_from, 0, first), (1, tok_rows, 2 * width))[0]

        own_share, their_share = share(*places[0:2]), swap(share(*places[2:4]))

    with jax.named_scope("slot_units"):

        def of_slot(chip_from, first):
            size = (1, core_rows, unit_width)
            return [
                lax.dynamic_slice(units, (chip_from, 0, first + part), size)[0]
                for part in (0, 2 * unit_width)
            ]

        mine = of_slot(*places[4:6]) + of_slot(*places[6:8])
        theirs = swap(jnp.concatenate(mine[2:] + mine[:2], axis=1))
        theirs = lax.optimization_barrier((theirs, own_result))[0]
        slot_units = jnp.concatenate([jnp.concatenate(mine, axis=1), theirs], axis=0).T
        own_units, other_units = slot_units[: 2 * unit_width], slot_units[2 * unit_width :]

    with jax.named_scope("all_rows"):
        pair = jnp.stack(lax.optimization_barrier((routed, rows_y, sent_rows))[:2])
        pairs = [pair] + [
            lax.ppermute(pair, "x", [(i, (i + s) % column) for i in range(column)])
            for s in range(1, column)
        ]

    with jax.named_scope("new_slices"):
        units_spec = pl.BlockSpec((2 * unit_width, slot_rows), lambda t: (0, 0))
        rows_spec = pl.BlockSpec((1, slot_rows, 2 * width), lambda t: (t, 0, 0))
        part_spec = pl.BlockSpec((2, unit_width, width), lambda t: (t, 0, 0))
        part = jax.ShapeDtypeStruct((chips // 2, unit_width, width), BF16)
        held = []
        for g in range(2):
            up_part, down_part, theirs = pl.pallas_call(
                gradient_kernel,
                grid=(2,),
                out_shape=(
                    part,
                    part,
                    jax.ShapeDtypeStruct((chips // 2, 2 * unit_width, width), BF16),
                ),
                in_specs=[units_spec, units_spec, rows_spec, rows_spec, ANY],
                out_specs=(
                    part_spec,
                    part_spec,
                    pl.BlockSpec((2, 2 * unit_width, width), lambda t: (t, 0, 0)),
                ),
                compiler_params=LARGE,
            )(own_units, other_units, *pairs[2 * g : 2 * g + 2], own_result)
            held += [up_part, down_part, swap(theirs)]
        grad = jax.ShapeDtypeStruct((unit_width, cut_count * width), BF16)
        up_grad, down_grad = pl.pallas_call(
            layout_kernel,
            out_shape=(grad, grad),
            in_specs=[pl.BlockSpec(memory_space=pltpu.SMEM)] + [VMEM] * 6,
            out_specs=(VMEM, VMEM),
            compiler_params=LARGE,
        )(source, *held)
        their_share, up_grad, down_grad = lax.optimization_barrier(
            (their_share, up_grad, down_grad)
        )
    result = (own_share.astype(F32) + their_share.astype(F32)).astype(BF16)
    return (result[:, :width], result[:, width:], up_grad, down_grad)


def solution(mesh):
    experts, cuts = mesh.devices.shape
    split = Mesh(mesh.devices.reshape(experts, 2, cuts // 4, 2), ("expert", "y", "x", "core"))
    spread = P("expert", CUTS)
    return jax.shard_map(
        local,
        mesh=split,
        in_specs=(spread, P("expert", None), P("expert", None), spread, spread, P(), P(), spread),
        out_specs=(
            spread,
            spread,
            P(("expert", *CUTS), None),
            P(("expert", *CUTS), None),
        ),
        check_vma=False,
    )
```

```python
import jax
import jax.numpy as jnp
from jax import lax
from jax.experimental import pallas as pl
from jax.experimental.pallas import tpu as pltpu
from jax.sharding import Mesh, PartitionSpec as P

F32, BF16 = jnp.float32, jnp.bfloat16
CHIP = ("y", "x")
CUTS = ("y", "x", "core")
VMEM = pl.BlockSpec(memory_space=pltpu.VMEM)
ANY = pl.BlockSpec(memory_space=pl.ANY)
LARGE = pltpu.CompilerParams(vmem_limit_bytes=24 * 2**20)


def exchange(parts, axis):
    return lax.all_to_all(parts, axis, split_axis=0, concat_axis=0, tiled=True)


def everywhere(block, axis):
    return exchange(jnp.broadcast_to(block[None], (lax.axis_size(axis), *block.shape)), axis)


def swap(block):
    return lax.ppermute(block, "core", [(0, 1), (1, 0)])


def pick(blocks, index):
    return lax.dynamic_index_in_dim(blocks, index, axis=0, keepdims=False)


def rows_at(blocks, places):
    return jnp.take(blocks, places, axis=0, mode="clip")


def joined(refs):
    return [
        jnp.concatenate([refs[i][...], refs[i + 1][...]], axis=0) for i in range(0, len(refs), 2)
    ]


def partial_kernel(slots_ref, rows_ref, *refs):
    weights, out_ref = joined(refs[:-1]), refs[-1]
    width = weights[0].shape[1]
    units = out_ref.shape[2] // 2
    for i in range(2):
        part = sum(
            lax.dot_general(
                rows_ref[:, (2 * i + j) * width : (2 * i + j + 1) * width],
                weights[2 * i + j],
                (((1,), (1,)), ((), ())),
                preferred_element_type=F32,
            )
            for j in range(2)
        )
        out_ref[0, :, i * units : (i + 1) * units] = part.astype(BF16)


def rows_kernel(slots_ref, units_ref, *refs):
    up, other_up, down, other_down = joined(refs[:-2])
    out_ref, total = refs[-2:]
    width = up.shape[1]
    count = units_ref.shape[2] // 2

    @pl.when(pl.program_id(0) == 0)
    def _():
        total[...] = jnp.zeros_like(total)

    hidden, pre_grad = units_ref[0, :, :count], units_ref[0, :, count:]
    products = ((hidden, down), (pre_grad, up), (hidden, other_down), (pre_grad, other_up))
    for i, (left, right) in enumerate(products):
        total[:, i * width : (i + 1) * width] += jnp.dot(
            left, right, preferred_element_type=F32
        )

    @pl.when(pl.program_id(0) == pl.num_programs(0) - 1)
    def _():
        out_ref[...] = total[...].astype(BF16)


def gradient_kernel(own_units, other_units, first, second, after_ref, up_ref, down_ref, theirs_ref):
    unit_width, width = up_ref.shape[1:]
    hidden, pre_grad = [
        jnp.concatenate([own_units[part], other_units[part]], axis=0)
        for part in (pl.ds(0, unit_width), pl.ds(unit_width, unit_width))
    ]
    for j, rows in enumerate((first, second)):
        up = jnp.dot(pre_grad, rows[0, :, :width], preferred_element_type=F32).astype(BF16)
        down = jnp.dot(hidden, rows[0, :, width:], preferred_element_type=F32).astype(BF16)
        up_ref[j] = up[:unit_width]
        down_ref[j] = down[:unit_width]
        theirs_ref[j, :unit_width] = up[unit_width:]
        theirs_ref[j, unit_width:] = down[unit_width:]


def layout_kernel(source_ref, *refs):
    held, (up_ref, down_ref), parts, sems = refs[:6], refs[6:8], refs[8:14], refs[14]
    copies = [
        pltpu.make_async_copy(held[i], parts[i], sems.at[i]) for i in range(len(held))
    ]
    for copy in copies:
        copy.start()
    for copy in copies:
        copy.wait()
    groups = (parts[:3], parts[3:])
    blocks, unit_width, width = parts[0].shape
    for p in range(4 * blocks):
        columns = pl.ds(p * width, width)
        source = source_ref[p]
        place = source % blocks
        for g, (own_up, own_down, theirs) in enumerate(groups):

            @pl.when(source // blocks == 2 * g)
            def _():
                up_ref[:, columns] = own_up[place]
                down_ref[:, columns] = own_down[place]

            @pl.when(source // blocks == 2 * g + 1)
            def _():
                up_ref[:, columns] = theirs[place, :unit_width]
                down_ref[:, columns] = theirs[place, unit_width:]


def local(tokens, expert_ids, gate_weights, old_up, old_down, old_rows, new_slots, cotangent):
    chips = lax.axis_size(CHIP)
    cut_count = 2 * chips
    group_count = lax.axis_size("expert")
    expert_count = group_count // 2
    tok_rows, width = tokens.shape
    half_units = old_up.shape[0]
    unit_width = half_units // cut_count
    capacity = 8 * tok_rows // group_count
    slot_rows = group_count * capacity
    chip, core = lax.axis_index(CHIP), lax.axis_index("core")
    cut, other_cut = 2 * chip + core, 2 * chip + 1 - core
    cut_list = jnp.arange(cut_count, dtype=jnp.int32)
    inverse = jnp.sum(
        cut_list[:, None] * (old_rows[:, None] == cut_list[None, :]).astype(jnp.int32), axis=0
    )

    with jax.named_scope("weights"):
        weights = [old_up, swap(old_up), old_down, swap(old_down)]

    def over_chips(kernel, first, first_spec, out_shape, out_spec, scratch=()):
        unit_specs = [
            pl.BlockSpec((unit_width, width), lambda p, slots, i=i: (slots[2 * p + i], 0))
            for i in range(2)
        ]
        return pl.pallas_call(
            kernel,
            grid_spec=pltpu.PrefetchScalarGridSpec(
                num_scalar_prefetch=1,
                grid=(chips,),
                in_specs=[first_spec] + unit_specs * 4,
                out_specs=out_spec,
                scratch_shapes=scratch,
            ),
            out_shape=out_shape,
        )(new_slots, first, *[half for block in weights for half in (block, block)])

    with jax.named_scope("token_blocks"):
        blocks = everywhere(jnp.concatenate([tokens, cotangent], axis=1), CUTS)
        own, other = pick(blocks, pick(old_rows, cut)), pick(blocks, pick(old_rows, other_cut))
        both = jnp.concatenate(
            [own[:, :width], other[:, :width], own[:, width:], other[:, width:]], axis=1
        )

    flat_ids = expert_ids.reshape(-1)
    expert_hits = (flat_ids[:, None] == jnp.arange(expert_count, dtype=jnp.int32)[None, :]).astype(
        jnp.int32
    )
    slot_rank = jnp.sum((jnp.cumsum(expert_hits, axis=0) - expert_hits) * expert_hits, axis=1)
    target = (flat_ids * capacity + slot_rank).reshape(tok_rows, 2)
    held_slots = capacity // 2
    core_rows = slot_rows // 2
    slot_list = 2 * jnp.arange(expert_count * held_slots, dtype=jnp.int32) + core
    matches = slot_list[:, None, None] == target[None]
    placer = jnp.any(matches, axis=2).astype(BF16)
    slot_gate = jnp.sum(jnp.where(matches, gate_weights[None], 0.0), axis=(1, 2))

    with jax.named_scope("dispatch"):
        placed = jnp.dot(placer, both, preferred_element_type=F32)
        scale = jnp.where(jnp.arange(4 * width)[None, :] < 2 * width, 1.0, slot_gate[:, None])
        placed = (placed * scale).astype(BF16).reshape(expert_count, 1, held_slots, 4 * width)
        placed = jnp.broadcast_to(placed, (expert_count, 2, held_slots, 4 * width))
        rows = exchange(placed.reshape(group_count, held_slots, 4 * width), "expert")
        rows = rows.reshape(core_rows, 4 * width)

    def found(place):
        source = pick(inverse, place)
        return source // 2, jnp.where(source % 2 == core, 0, 2 * width)

    column = lax.axis_size("x")
    source = inverse // 2
    back = (lax.axis_index("x") - source % column) % column
    other_y = (source // column != lax.axis_index("y")).astype(jnp.int32)
    other_core = (inverse % 2 != core).astype(jnp.int32)
    source = 8 * (back // 2) + 4 * other_core + 2 * other_y + back % 2
    row_list = jnp.arange(core_rows, dtype=jnp.int32)
    row_slot = row_list // capacity * capacity + row_list % held_slots * 2 + core
    picker = (target.reshape(-1)[:, None] == row_slot[None, :]).astype(BF16)
    places = [*found(cut), *found(other_cut)]
    rows, source, picker, places = lax.optimization_barrier((rows, source, picker, places))

    with jax.named_scope("hidden"):
        parts = over_chips(
            partial_kernel,
            rows,
            pl.BlockSpec((core_rows, 4 * width), lambda p, slots: (0, 0)),
            jax.ShapeDtypeStruct((chips, core_rows, 4 * unit_width), BF16),
            pl.BlockSpec((1, core_rows, 4 * unit_width), lambda p, slots: (p, 0, 0)),
        )
        sums = jnp.sum(exchange(parts, CHIP).astype(F32), axis=0)
        pre_act, hidden_grad = sums[:, : 2 * unit_width], sums[:, 2 * unit_width :]
        sig = jax.nn.sigmoid(pre_act)
        hidden = jax.nn.silu(pre_act).astype(BF16)
        pre_grad = (hidden_grad * sig * (1.0 + pre_act * (1.0 - sig))).astype(BF16)
        own_units = jnp.concatenate([hidden, pre_grad], axis=1)

        others = swap(
            jnp.concatenate([rows[:, width : 2 * width], rows[:, 3 * width :]], axis=1)
        )
        routed = jnp.concatenate([rows[:, :width], rows[:, 2 * width : 3 * width]], axis=1)
        routed = jnp.concatenate([routed, others], axis=0)
        later_rows, own_units = lax.optimization_barrier((routed, own_units))
        rows_y = lax.ppermute(later_rows, "y", [(0, 1), (1, 0)])
        halves = [own_units[:, i * unit_width : (i + 1) * unit_width] for i in range(4)]
        mine = [jnp.where(core == 0, halves[i], halves[i + 1]) for i in (0, 2)]
        mine += [jnp.where(core == 0, halves[i + 1], halves[i]) for i in (0, 2)]
        theirs = swap(jnp.concatenate(mine[2:] + mine[:2], axis=1))
        slot_units = jnp.concatenate([jnp.concatenate(mine, axis=1), theirs], axis=0).T
        units = everywhere(own_units, CHIP)
        units, rows_y, slot_units = lax.optimization_barrier((units, rows_y, slot_units))

    with jax.named_scope("give_back"):
        half_rows = over_chips(
            rows_kernel,
            units,
            pl.BlockSpec((1, core_rows, 4 * unit_width), lambda p, slots: (p, 0, 0)),
            jax.ShapeDtypeStruct((core_rows, 4 * width), BF16),
            pl.BlockSpec((core_rows, 4 * width), lambda p, slots: (0, 0)),
            [pltpu.VMEM((core_rows, 4 * width), F32)],
        )
        sent_rows = half_rows.reshape(group_count, held_slots, 4 * width)
        half_rows = exchange(sent_rows, "expert")
        entries = jnp.dot(picker, half_rows.reshape(core_rows, 4 * width), preferred_element_type=F32)
        is_out = jnp.arange(4 * width) // width % 2 == 0
        factor = jnp.where(is_out[None, None, :], gate_weights[:, :, None], 1.0)
        own_result = jnp.sum(entries.reshape(tok_rows, 2, 4 * width) * factor, axis=1).astype(BF16)

    with jax.named_scope("result"):
        got = everywhere(own_result, CHIP)

        def share(chip_from, first):
            return lax.dynamic_slice(got, (chip_from, 0, first), (1, tok_rows, 2 * width))[0]

        own_share, their_share = share(*places[0:2]), swap(share(*places[2:4]))

    with jax.named_scope("all_rows"):
        pair = jnp.stack(lax.optimization_barrier((routed, rows_y, sent_rows))[:2])
        pairs = [pair] + [
            lax.ppermute(pair, "x", [(i, (i + s) % column) for i in range(column)])
            for s in range(1, column)
        ]

    with jax.named_scope("new_slices"):
        own_units, other_units = slot_units[: 2 * unit_width], slot_units[2 * unit_width :]
        units_spec = pl.BlockSpec((2 * unit_width, slot_rows), lambda t: (0, 0))
        rows_spec = pl.BlockSpec((1, slot_rows, 2 * width), lambda t: (t, 0, 0))
        part_spec = pl.BlockSpec((2, unit_width, width), lambda t: (t, 0, 0))
        part = jax.ShapeDtypeStruct((chips // 2, unit_width, width), BF16)
        held = []
        for g in range(2):
            up_part, down_part, theirs = pl.pallas_call(
                gradient_kernel,
                grid=(2,),
                out_shape=(
                    part,
                    part,
                    jax.ShapeDtypeStruct((chips // 2, 2 * unit_width, width), BF16),
                ),
                in_specs=[units_spec, units_spec, rows_spec, rows_spec, ANY],
                out_specs=(
                    part_spec,
                    part_spec,
                    pl.BlockSpec((2, 2 * unit_width, width), lambda t: (t, 0, 0)),
                ),
                compiler_params=LARGE,
            )(own_units, other_units, *pairs[2 * g : 2 * g + 2], own_result)
            held += [up_part, down_part, swap(theirs)]
        grad = jax.ShapeDtypeStruct((unit_width, cut_count * width), BF16)
        up_grad, down_grad = pl.pallas_call(
            layout_kernel,
            out_shape=(grad, grad),
            in_specs=[pl.BlockSpec(memory_space=pltpu.SMEM)] + [ANY] * 6,
            out_specs=(VMEM, VMEM),
            scratch_shapes=[pltpu.VMEM(part.shape, BF16) for part in held]
            + [pltpu.SemaphoreType.DMA((6,))],
            compiler_params=LARGE,
        )(source, *held)
        their_share, up_grad, down_grad = lax.optimization_barrier(
            (their_share, up_grad, down_grad)
        )
    result = (own_share.astype(F32) + their_share.astype(F32)).astype(BF16)
    return (result[:, :width], result[:, width:], up_grad, down_grad)


def solution(mesh):
    experts, cuts = mesh.devices.shape
    split = Mesh(mesh.devices.reshape(experts, 2, cuts // 4, 2), ("expert", "y", "x", "core"))
    spread = P("expert", CUTS)
    return jax.shard_map(
        local,
        mesh=split,
        in_specs=(spread, P("expert", None), P("expert", None), spread, spread, P(), P(), spread),
        out_specs=(
            spread,
            spread,
            P(("expert", *CUTS), None),
            P(("expert", *CUTS), None),
        ),
        check_vma=False,
    )
```

```python
import jax
import jax.numpy as jnp
from jax import lax
from jax.experimental import pallas as pl
from jax.experimental.pallas import tpu as pltpu
from jax.sharding import Mesh, PartitionSpec as P

F32, BF16 = jnp.float32, jnp.bfloat16
CHIP = ("y", "x")
CUTS = ("y", "x", "core")
VMEM = pl.BlockSpec(memory_space=pltpu.VMEM)
ANY = pl.BlockSpec(memory_space=pl.ANY)
LARGE = pltpu.CompilerParams(vmem_limit_bytes=8 * 2**20)


def exchange(parts, axis):
    return lax.all_to_all(parts, axis, split_axis=0, concat_axis=0, tiled=True)


def everywhere(block, axis):
    return exchange(jnp.broadcast_to(block[None], (lax.axis_size(axis), *block.shape)), axis)


def swap(block):
    return lax.ppermute(block, "core", [(0, 1), (1, 0)])


def pick(blocks, index):
    return lax.dynamic_index_in_dim(blocks, index, axis=0, keepdims=False)


def rows_at(blocks, places):
    return jnp.take(blocks, places, axis=0, mode="clip")


def gradient_kernel(own_units, other_units, *refs):
    rows, (own_ref, theirs_ref) = refs[:-3], refs[-2:]
    unit_width = own_units.shape[0]
    units = jnp.concatenate([own_units[...], other_units[...]], axis=0)
    for s, block in enumerate(rows):
        grad = jnp.dot(units, block[...], preferred_element_type=F32).astype(BF16)
        own_ref[0, s] = grad[:unit_width]
        theirs_ref[0, s] = grad[unit_width:]


def layout_kernel(source_ref, *refs):
    held, outs = refs[:-2], refs[-2:]
    _, blocks, _, width = held[0].shape
    for p in range(len(held) * blocks):
        source = source_ref[p]
        for g, part in enumerate(held):

            @pl.when(source // blocks == g)
            def _():
                for i, out_ref in enumerate(outs):
                    out_ref[:, p * width : (p + 1) * width] = part[i, source % blocks]


def local(tokens, expert_ids, gate_weights, old_up, old_down, old_rows, new_slots, cotangent):
    chips = lax.axis_size(CHIP)
    cut_count = 2 * chips
    group_count = lax.axis_size("expert")
    expert_count = group_count // 2
    tok_rows, width = tokens.shape
    half_units = old_up.shape[0]
    unit_width = half_units // cut_count
    capacity = 8 * tok_rows // group_count
    slot_rows = group_count * capacity
    chip, core = lax.axis_index(CHIP), lax.axis_index("core")
    cut, other_cut = 2 * chip + core, 2 * chip + 1 - core
    cut_list = jnp.arange(cut_count, dtype=jnp.int32)
    inverse = jnp.sum(
        cut_list[:, None] * (old_rows[:, None] == cut_list[None, :]).astype(jnp.int32), axis=0
    )

    with jax.named_scope("weights"):
        shape = (chips, 2 * unit_width, width)
        up = [old_up.reshape(shape), swap(old_up).reshape(shape)]
        down = [old_down.reshape(shape), swap(old_down).reshape(shape)]

    with jax.named_scope("token_blocks"):
        blocks = everywhere(jnp.concatenate([tokens, cotangent], axis=1), CUTS)
        own, other = pick(blocks, pick(old_rows, cut)), pick(blocks, pick(old_rows, other_cut))
        both = jnp.concatenate(
            [own[:, :width], other[:, :width], own[:, width:], other[:, width:]], axis=1
        )

    flat_ids = expert_ids.reshape(-1)
    expert_hits = (flat_ids[:, None] == jnp.arange(expert_count, dtype=jnp.int32)[None, :]).astype(
        jnp.int32
    )
    slot_rank = jnp.sum((jnp.cumsum(expert_hits, axis=0) - expert_hits) * expert_hits, axis=1)
    target = (flat_ids * capacity + slot_rank).reshape(tok_rows, 2)
    held_slots = capacity // 2
    core_rows = slot_rows // 2
    slot_list = 2 * jnp.arange(expert_count * held_slots, dtype=jnp.int32) + core
    matches = slot_list[:, None, None] == target[None]
    placer = jnp.any(matches, axis=2).astype(BF16)
    slot_gate = jnp.sum(jnp.where(matches, gate_weights[None], 0.0), axis=(1, 2))

    with jax.named_scope("dispatch"):
        placed = jnp.dot(placer, both, preferred_element_type=F32)
        scale = jnp.where(jnp.arange(4 * width)[None, :] < 2 * width, 1.0, slot_gate[:, None])
        placed = (placed * scale).astype(BF16).reshape(expert_count, 1, held_slots, 4 * width)
        placed = jnp.broadcast_to(placed, (expert_count, 2, held_slots, 4 * width))
        rows = exchange(placed.reshape(group_count, held_slots, 4 * width), "expert")
        rows = rows.reshape(core_rows, 4 * width)

    def found(place):
        source = pick(inverse, place)
        return source // 2, jnp.where(source % 2 == core, 0, 2 * width)

    def slot(place):
        block = pick(new_slots, place)
        return block // 2, block % 2 * unit_width

    column = lax.axis_size("x")
    source = inverse // 2
    back = (lax.axis_index("x") - source % column) % column
    other_y = (source // column != lax.axis_index("y")).astype(jnp.int32)
    other_core = (inverse % 2 != core).astype(jnp.int32)
    source = (2 * other_y + other_core) * column + back
    row_list = jnp.arange(core_rows, dtype=jnp.int32)
    row_slot = row_list // capacity * capacity + row_list % held_slots * 2 + core
    picker = (target.reshape(-1)[:, None] == row_slot[None, :]).astype(BF16)
    places = [*found(cut), *found(other_cut), *slot(cut), *slot(other_cut)]
    rows, source, picker, places = lax.optimization_barrier((rows, source, picker, places))

    def partial(weights, first):
        return sum(
            jnp.einsum(
                "rd,pud->pru",
                rows[:, first + j * width : first + (j + 1) * width],
                weights[j],
                preferred_element_type=F32,
            )
            for j in range(2)
        ).astype(BF16)

    with jax.named_scope("hidden"):
        parts = jnp.concatenate([partial(up, 0), partial(down, 2 * width)], axis=2)
        sums = jnp.sum(exchange(parts, CHIP).astype(F32), axis=0)
        pre_act, hidden_grad = sums[:, : 2 * unit_width], sums[:, 2 * unit_width :]
        sig = jax.nn.sigmoid(pre_act)
        hidden = jax.nn.silu(pre_act).astype(BF16)
        pre_grad = (hidden_grad * sig * (1.0 + pre_act * (1.0 - sig))).astype(BF16)
        own_units = jnp.concatenate([hidden, pre_grad], axis=1)

        others = swap(
            jnp.concatenate([rows[:, width : 2 * width], rows[:, 3 * width :]], axis=1)
        )
        routed = jnp.concatenate([rows[:, :width], rows[:, 2 * width : 3 * width]], axis=1)
        routed = jnp.concatenate([routed, others], axis=0)
        units = everywhere(own_units, CHIP)
        hidden, pre_grad = units[:, :, : 2 * unit_width], units[:, :, 2 * unit_width :]

    def rows_of(units, weights):
        return jnp.einsum("pru,pud->rd", units, weights, preferred_element_type=F32).astype(BF16)

    with jax.named_scope("give_back"):
        half_rows = jnp.concatenate(
            [rows_of(part, weights[j]) for j in range(2) for part, weights in ((hidden, down), (pre_grad, up))],
            axis=1,
        )
        sent_rows = half_rows.reshape(group_count, held_slots, 4 * width)
        half_rows = exchange(sent_rows, "expert")

        def along_x(start):
            return [start] + [
                lax.ppermute(start, "x", [(i, (i + s) % column) for i in range(column)])
                for s in range(1, column)
            ]

        own_y = lax.optimization_barrier((routed, sent_rows))[0]
        all_rows = [along_x(own_y), along_x(lax.ppermute(own_y, "y", [(0, 1), (1, 0)]))]
        half_rows, all_rows = lax.optimization_barrier((half_rows, all_rows))
        entries = jnp.dot(picker, half_rows.reshape(core_rows, 4 * width), preferred_element_type=F32)
        is_out = jnp.arange(4 * width) // width % 2 == 0
        factor = jnp.where(is_out[None, None, :], gate_weights[:, :, None], 1.0)
        own_result = jnp.sum(entries.reshape(tok_rows, 2, 4 * width) * factor, axis=1).astype(BF16)

    with jax.named_scope("result"):
        got = everywhere(own_result, CHIP)

        def share(chip_from, first):
            return lax.dynamic_slice(got, (chip_from, 0, first), (1, tok_rows, 2 * width))[0]

        own_share, their_share = share(*places[0:2]), swap(share(*places[2:4]))

    with jax.named_scope("slot_units"):

        def of_slot(chip_from, first):
            size = (1, core_rows, unit_width)
            return [
                lax.dynamic_slice(units, (chip_from, 0, first + part), size)[0]
                for part in (0, 2 * unit_width)
            ]

        mine = of_slot(*places[4:6]) + of_slot(*places[6:8])
        theirs = swap(jnp.concatenate(mine[2:] + mine[:2], axis=1))
        theirs = lax.optimization_barrier((theirs, own_result))[0]
        slot_units = jnp.concatenate([jnp.concatenate(mine, axis=1), theirs], axis=0).T
        own_units, other_units = slot_units[: 2 * unit_width], slot_units[2 * unit_width :]

    with jax.named_scope("new_slices"):
        units_spec = pl.BlockSpec((unit_width, slot_rows), lambda t: (1 - t, 0))
        rows_spec = pl.BlockSpec((slot_rows, width), lambda t: (0, t))
        part_spec = pl.BlockSpec((1, column, unit_width, width), lambda t: (t, 0, 0, 0))
        part = jax.ShapeDtypeStruct((2, column, unit_width, width), BF16)
        held = []
        for rows in all_rows:
            own, theirs = pl.pallas_call(
                gradient_kernel,
                grid=(2,),
                out_shape=(part, part),
                in_specs=[units_spec] * 2 + [rows_spec] * column + [ANY],
                out_specs=(part_spec, part_spec),
                compiler_params=LARGE,
            )(own_units, other_units, *rows, own_result)
            held += [own, swap(theirs)]
        grad = jax.ShapeDtypeStruct((unit_width, cut_count * width), BF16)
        up_grad, down_grad = pl.pallas_call(
            layout_kernel,
            out_shape=(grad, grad),
            in_specs=[pl.BlockSpec(memory_space=pltpu.SMEM)] + [VMEM] * 4,
            out_specs=(VMEM, VMEM),
            compiler_params=LARGE,
        )(source, *held)
        their_share, up_grad, down_grad = lax.optimization_barrier(
            (their_share, up_grad, down_grad)
        )
    result = (own_share.astype(F32) + their_share.astype(F32)).astype(BF16)
    return (result[:, :width], result[:, width:], up_grad, down_grad)


def solution(mesh):
    experts, cuts = mesh.devices.shape
    split = Mesh(mesh.devices.reshape(experts, 2, cuts // 4, 2), ("expert", "y", "x", "core"))
    spread = P("expert", CUTS)
    return jax.shard_map(
        local,
        mesh=split,
        in_specs=(spread, P("expert", None), P("expert", None), spread, spread, P(), P(), spread),
        out_specs=(
            spread,
            spread,
            P(("expert", *CUTS), None),
            P(("expert", *CUTS), None),
        ),
        check_vma=False,
    )
```
